512 devices in a mesh: band: 32 (over y, x, core), work: 16 (over z).
Axes of the slice: x: 4, y: 4, z: 16, core: 2. Of those that a mesh axis runs over, the one named last changes fastest.
Arguments:
- mask_logits: float32 [1536, 4096], P('band', 'work'), may hold values from -6 to 6
- loss_weights: float32 [1536, 4096], P('band', 'work'), may hold values from 0.1 to 6, as said below
- target_bits: int32 [1536, 4096], P('band', 'work'), may hold values 0 or 1
- kernels: bfloat16 [24, 25, 25], replicated, may hold values from -0.25 to 0.25
- kernel_gains: float32 [12], replicated, may hold values from 0.02 to 0.2
- imager_list: int32 [32, 16, 2, 1], P('band'), may hold values from 0 to 16, as said below
Outputs:
- final_logits: float32 [1536, 4096], P('band', 'work')
The draws below stay inside these ranges and needn't reach their ends.
Inputs may be any that keep to these rules, and one draw needn't show every extreme that they name: `imager_list`: an entry 16 marks a tile without pattern, which is not imaged; in every row group some device has both its tiles with pattern. `loss_weights`: positive weights.
All inputs are finite; a program needn't handle non-finite values. No bound on the sum of `target_bits` on one device may be relied on, other than what follows from the above.
Results may differ from the reference program's by a relative error of at most 0.0045.
Values may be sent and summed in bfloat16 or wider, within the bound.
A program may use at most 64 MiB of HBM per device.

```python
import math
import jax
import jax.numpy as jnp
from jax import lax

K = 12
KS = 25
TR = 24
TC = 256
TPD = 2
ITERS = 2
ROWS = 1536
COLS = 4096
N_BAND = 32
N_WORK = 16


def draw_loss_weights(key, part):
    key = jax.random.fold_in(key, 5)
    row_ids = lax.broadcasted_iota(jnp.int32, (ROWS, COLS), 0)
    col_ids = lax.broadcasted_iota(jnp.int32, (ROWS, COLS), 1)
    block_rows = TPD * TR
    rim_width = (KS - 1) // 2
    row_inside = row_ids % block_rows
    col_inside = col_ids % TC
    near_edge = jnp.logical_or(jnp.logical_or(row_inside < rim_width, row_inside >= block_rows - rim_width), jnp.logical_or(col_inside < rim_width, col_inside >= TC - rim_width))
    row_place = row_ids.astype(jnp.float32) / ROWS
    col_place = col_ids.astype(jnp.float32) / COLS
    fraction = jax.random.uniform(key, (ROWS, COLS), jnp.float32, 0.0, 1.0)
    edge_log = math.log(2.0) + (math.log(3.0) - math.log(2.0)) * fraction
    inner_log = math.log(0.28) + (math.log(0.4) - math.log(0.28)) * fraction
    values = jnp.exp(jnp.where(near_edge, edge_log, inner_log))
    return values * (0.6 + 0.8 * row_place) * (0.6 + 0.8 * col_place)


def draw_imager_list(key, part):
    key = jax.random.fold_in(key, 11)
    key_shift, key_full, key_perm, key_offset = jax.random.split(key, 4)
    shifts = jax.random.randint(key_shift, (N_BAND, N_WORK), 0, 4)
    counts = jnp.maximum(jnp.right_shift(jnp.full((N_BAND, N_WORK), TPD, jnp.int32), shifts), 1)
    full_at = jax.random.randint(key_full, (N_BAND, 1), 0, N_WORK)
    columns = lax.broadcasted_iota(jnp.int32, (N_BAND, N_WORK), 1)
    counts = jnp.where(columns == full_at, TPD, counts)
    perm_keys = jax.random.split(key_perm, N_BAND * N_WORK)
    tile_ranks = jax.vmap(lambda subkey: jax.random.permutation(subkey, TPD))(perm_keys).reshape(N_BAND, N_WORK, TPD)
    offsets = jax.random.randint(key_offset, (N_BAND, N_WORK, 1), 0, N_WORK)
    live_tiles = tile_ranks < counts[:, :, None]
    imager_ids = jnp.where(live_tiles, (offsets + tile_ranks) % N_WORK, N_WORK)
    return imager_ids[:, :, :, None].astype(jnp.int32)


def touch_ends(drawn, stream_key, low, largest):
    place = [jax.random.randint(jax.random.fold_in(stream_key, axis), (), 0, length) for axis, length in enumerate(drawn.shape)]
    main_axis = drawn.shape.index(max(drawn.shape))
    next_to = place[:main_axis] + [(place[main_axis] + 1) % drawn.shape[main_axis]] + place[main_axis + 1:]
    return drawn.at[tuple(place)].set(low).at[tuple(next_to)].set(largest)


def level_of(key, shape, shards, low, top_value):
    loudness = 1.0
    for axis_at, blocks in shards:
        heights = jax.random.uniform(jax.random.fold_in(jax.random.fold_in(key, 6), axis_at), (blocks,), jnp.float32, low / len(shards), top_value / len(shards))
        loudness = loudness * jnp.repeat(jnp.exp(heights), shape[axis_at] // blocks).reshape((-1,) + (1,) * (len(shape) - 1 - axis_at))
    return loudness


def gaussian(key, extent, deviation, reach, cuts=(), kind=jnp.bfloat16):
    entries = jax.random.normal(key, extent, jnp.float32) * deviation
    if len(cuts) > 0:
        entries = level_of(key, extent, cuts, -0.22, 0.18) * entries
    return jnp.clip(entries, min=-reach, max=reach).astype(kind)


def setup_inputs(seed: int = 0) -> dict:
    key_list = jax.random.split(jax.random.key(seed), 7)
    return {
        "mask_logits": gaussian(key_list[0], (ROWS, COLS), 1.5, 6.0, ((0, 32), (1, 16)), jnp.float32),
        "loss_weights": draw_loss_weights(jax.random.fold_in(key_list[6], 71), 0),
        "target_bits": touch_ends((jax.random.randint(key_list[2], (ROWS, COLS), 0, 2) < 1).astype(jnp.int32), jax.random.fold_in(key_list[2], 1), 0, 1),
        "kernels": gaussian(key_list[3], (2 * K, KS, KS), (KS * KS) ** -0.5, 0.25),
        "kernel_gains": jnp.clip(jnp.exp(jax.random.uniform(key_list[4], (K,), jnp.float32, math.log(0.02), math.log(0.2))), 0.02, 0.2),
        "imager_list": draw_imager_list(jax.random.fold_in(key_list[6], 71), 0),
    }


STEEP = 4.0
THRESH = 0.5
STEP_SIZE = 0.5
EPSILON = 1e-06

def kernel_spectrum(kernel, shape):
    framed = jnp.zeros(shape, jnp.float32).at[:kernel.shape[0], :kernel.shape[1]].set(kernel)
    spectrum = jnp.fft.rfft2(framed)
    return (jnp.real(spectrum), jnp.imag(spectrum))

def reference(mask_logits, loss_weights, target_bits, kernels, kernel_gains, imager_list):
    kernel_taps = kernels.shape[1]
    halo_width = (kernel_taps - 1) // 2
    total_rows, total_cols = mask_logits.shape
    shape = (total_rows + 2 * halo_width, total_cols + 2 * halo_width)
    live_tiles = (imager_list[:, :, :, 0] < N_WORK).astype(jnp.float32)
    live_tiles = jnp.transpose(live_tiles, (0, 2, 1))
    live_pixels = jnp.broadcast_to(live_tiles[:, :, None, :, None], (N_BAND, TPD, TR, N_WORK, TC)).reshape(total_rows, total_cols)
    weight_v = loss_weights.astype(jnp.bfloat16).astype(jnp.float32)
    weight_t = weight_v * target_bits.astype(jnp.float32)
    sigma_both = jnp.concatenate([kernel_gains, kernel_gains])
    spec_real, spec_imag = lax.map(lambda kernel: kernel_spectrum(kernel, shape), kernels.astype(jnp.float32))
    logits = mask_logits
    for iteration in range(ITERS):
        soft = jax.nn.sigmoid(logits)
        mask = soft.astype(jnp.bfloat16).astype(jnp.float32)
        mask_spec = jnp.fft.rfft2(jnp.pad(mask, halo_width))

        def correlate(pair):
            return jnp.fft.irfft2(mask_spec * lax.complex(pair[0], -pair[1]), s=shape)[:total_rows, :total_cols]
        fields = lax.map(correlate, (spec_real, spec_imag))
        intensity = lax.optimization_barrier(jnp.sum(sigma_both[:, None, None] * fields * fields, axis=0))
        resist = jax.nn.sigmoid(STEEP * (intensity - THRESH))
        slopes = 2.0 * (weight_v * resist - weight_t) * STEEP * resist * (1.0 - resist) * live_pixels
        field_grad = (2.0 * sigma_both[:, None, None] * fields * slopes).astype(jnp.bfloat16)

        def accumulate(carry, item):
            channel, kre, kim = item
            spectrum = jnp.fft.rfft2(jnp.pad(channel.astype(jnp.float32), ((0, 2 * halo_width), (0, 2 * halo_width))))
            sre = jnp.real(spectrum)
            sim = jnp.imag(spectrum)
            return ((carry[0] + sre * kre - sim * kim, carry[1] + sre * kim + sim * kre), None)
        zeros = jnp.zeros(spec_real.shape[1:], jnp.float32)
        (acc_real, acc_imag), unused = lax.scan(accumulate, (zeros, zeros), (field_grad, spec_real, spec_imag))
        whole = jnp.fft.irfft2(lax.complex(acc_real, acc_imag), s=shape)
        gradient = whole[halo_width:halo_width + total_rows, halo_width:halo_width + total_cols] * soft * (1.0 - soft)
        logits = logits - STEP_SIZE / jnp.sqrt(jnp.mean(gradient * gradient) + EPSILON) * gradient
    return logits
```

```python
import functools

import jax
import jax.numpy as jnp
from jax import lax
from jax.experimental import pallas as pl
from jax.experimental.pallas import tpu as pltpu
from jax.sharding import PartitionSpec as P

MESH = pl.DeviceIdType.MESH
TR = 24
H, W = 48, 256
K2 = 24
KS = 25
JP = 26
HALO = 24
ER, EC = 72, 384
LR, LC = 96, 512
OWN_R, OWN_C = 24, 128
KF = 4 * JP * 8
KFP = 896
KB = 4 * K2 * 8
ITERS = 2
STEEP, THRESH, STEP_SIZE, EPSILON = 4.0, 0.5, 0.5, 1e-6


def sigmoid(x):
    return 1.0 / (1.0 + jnp.exp(-x))


def kernel(
    nb, nw, log_ref, lw_ref, bits_ref, kf_ref, kb_ref, gain_ref, img_ref, out_ref,
    frame, gframe, vown, vframe, vext, tmat, umat, sblk, gblk, slots_c, slots_b, slots_w, part,
    a_send, a_recv, v_send, v_recv, g_send, g_recv, r_send, r_recv,
):
    b, w = lax.axis_index("band"), lax.axis_index("work")
    up, down = lax.rem(b + nb - 1, nb), lax.rem(b + 1, nb)
    left, right = lax.rem(w + nw - 1, nw), lax.rem(w + 1, nw)

    core = lax.rem(b, 2)

    def other_core(k):
        return (b + 1 - 2 * core, w)

    def same_core(k):
        return (lax.rem(b + 2 * k, nb), w)

    def along_work(k):
        return (b, lax.rem(w + k, nw))

    barrier = pltpu.get_barrier_semaphore()
    greeted = [along_work(k) for k in range(1, nw)] + [same_core(k) for k in range(1, nb // 2)]
    greeted += [(up, w), (down, w), (up, left), (up, right), (down, left), (down, right)]
    for dev in greeted:
        pl.semaphore_signal(barrier, inc=1, device_id=dev, device_id_type=MESH)

    rows = lax.broadcasted_iota(jnp.int32, (H, W), 0)
    live0 = jnp.where(img_ref[w * 2] < nw, 1.0, 0.0)
    live1 = jnp.where(img_ref[w * 2 + 1] < nw, 1.0, 0.0)
    weight = lw_ref[...].astype(jnp.bfloat16).astype(jnp.float32)
    weight = weight * jnp.where(rows < TR, live0, live1)
    vown[...] = jnp.where(bits_ref[...] == 1, -weight, weight).astype(jnp.bfloat16)

    pl.semaphore_wait(barrier, len(greeted))

    def frames(src, dst, h, top, send, recv):
        lo, hi = slice(0, h), slice(H - h, H)
        first, last = slice(0, 128), slice(W - 128, W)
        above, below = slice(top - h, top), slice(top + H, top + H + h)
        mid = slice(top, top + H)
        before, after, centre = slice(0, 128), slice(128 + W, 256 + W), slice(128, 128 + W)
        plan = (
            (lo, slice(0, W), below, centre, (up, w)),
            (hi, slice(0, W), above, centre, (down, w)),
            (slice(0, H), first, mid, after, (b, left)),
            (slice(0, H), last, mid, before, (b, right)),
            (lo, first, below, after, (up, left)),
            (lo, last, below, before, (up, right)),
            (hi, first, above, after, (down, left)),
            (hi, last, above, before, (down, right)),
        )
        copies = []
        for k, (sr, sc, dr, dc, dev) in enumerate(plan):
            copies.append(
                pltpu.make_async_remote_copy(
                    src.at[sr, sc], dst.at[dr, dc], send.at[k], recv.at[k], dev, MESH
                )
            )
        for copy in copies:
            copy.start()
        return copies

    copies_v = frames(vown, vframe, 16, 16, v_send, v_recv)
    copies_a = frames(log_ref, frame, HALO, OWN_R, a_send, a_recv)
    frame[OWN_R : OWN_R + H, OWN_C : OWN_C + W] = log_ref[...]
    vframe[16 : 16 + H, 128 : 128 + W] = vown[...]

    lane_f = lax.broadcasted_iota(jnp.int32, (8, KFP), 1) & 7
    sub_f = lax.broadcasted_iota(jnp.int32, (8, KFP), 0)
    lane_b = lax.broadcasted_iota(jnp.int32, (8, KB), 1) & 7
    sub_b = lax.broadcasted_iota(jnp.int32, (8, KB), 0)

    def toeplitz(row, lane, sub, step):
        wide = jnp.broadcast_to(row.astype(jnp.float32), lane.shape)
        same = pltpu.roll(wide, 0, 1, stride=1, stride_axis=0)
        prior = pltpu.roll(wide, step - 8, 1, stride=1, stride_axis=0)
        return jnp.where(lane >= sub, same, prior)

    for c in range(0, K2, 2):
        pair = [toeplitz(kf_ref[c + d : c + d + 1, :], lane_f, sub_f, JP * 8) for d in range(2)]
        tmat[8 * c : 8 * c + 16, :] = jnp.concatenate(pair, axis=0)[:, :KF].astype(jnp.bfloat16)
    for j in range(0, JP, 2):
        pair = [toeplitz(kb_ref[j + d : j + d + 1, :], lane_b, sub_b, K2 * 8) for d in range(2)]
        umat[8 * j : 8 * j + 16, :] = jnp.concatenate(pair, axis=0).astype(jnp.bfloat16)

    for copy in copies_v:
        copy.wait_recv()
    band_row = b * H + lax.broadcasted_iota(jnp.int32, (ER, EC), 0) - 12
    band_col = w * W + lax.broadcasted_iota(jnp.int32, (ER, EC), 1) - 12
    inside = (band_row >= 0) & (band_row < nb * H) & (band_col >= 0) & (band_col < nw * W)
    signed = vframe[...].astype(jnp.float32)
    signed = pltpu.roll(signed, LC - 116, 1)[4 : 4 + ER, :EC]
    vext[...] = jnp.where(inside, signed, 0.0)

    for copy in copies_a:
        copy.wait_recv()

    band_row = b * H + lax.broadcasted_iota(jnp.int32, (LR, LC), 0) - OWN_R
    band_col = w * W + lax.broadcasted_iota(jnp.int32, (LR, LC), 1) - OWN_C
    inside = (band_row >= 0) & (band_row < nb * H) & (band_col >= 0) & (band_col < nw * W)

    sends = list(copies_v) + list(copies_a)
    for step in range(ITERS):
        soft = sigmoid(frame[...])
        own_soft = soft[OWN_R : OWN_R + H, OWN_C : OWN_C + W]
        mask = jnp.where(inside, soft.astype(jnp.bfloat16).astype(jnp.float32), 0.0)
        for j in range(0, JP, 2):
            pair = [
                pltpu.roll(mask, LC - 104 - min(j + d, KS - 1), 1)[:, :EC].reshape(LR // 8, 8, EC)
                for d in range(2)
            ]
            sblk[:, 8 * j : 8 * j + 16, :] = jnp.concatenate(pair, axis=1).astype(jnp.bfloat16)

        def forward(blk, carry):
            window = sblk[pl.ds(blk, 4)].reshape(KF, EC)
            fields = jnp.dot(tmat[...], window, preferred_element_type=jnp.float32)
            fields = fields.reshape(K2, 8, EC)
            intensity = jnp.zeros((8, EC), jnp.float32)
            for c in range(K2 // 2):
                f0, f1 = fields[c], fields[c + K2 // 2]
                intensity = intensity + gain_ref[c] * (f0 * f0 + f1 * f1)
            resist = sigmoid(STEEP * (intensity - THRESH))
            v = vext[pl.ds(pl.multiple_of(blk * 8, 8), 8), :]
            target = jnp.where(v < 0.0, 1.0, 0.0)
            slopes = (8.0 * jnp.abs(v)) * (resist - target) * resist * (1.0 - resist)
            for c in range(0, K2, 2):
                pair = [2.0 * gain_ref[(c + d) % (K2 // 2)] * fields[c + d] * slopes for d in range(2)]
                gblk[blk, 8 * c : 8 * c + 16, :] = jnp.concatenate(pair, axis=0).astype(jnp.bfloat16)
            return carry

        lax.fori_loop(0, ER // 8, forward, 0)

        def backward(blk, carry):
            window = gblk[pl.ds(blk, 4)].reshape(KB, EC)
            spread = jnp.dot(umat[...], window, preferred_element_type=jnp.float32)
            spread = spread.reshape(JP, 8, EC)
            total = jnp.zeros((8, W), jnp.float32)
            for j in range(KS):
                shift = (EC - (KS - 1 - j)) % EC
                total = total + pltpu.roll(spread[j], shift, 1)[:, :W]
            at = pl.ds(pl.multiple_of(OWN_R + blk * 8, 8), 8)
            gframe[step, at, OWN_C : OWN_C + W] = total
            return carry

        lax.fori_loop(0, H // 8, backward, 0)

        own = gframe.at[step, OWN_R : OWN_R + H, OWN_C : OWN_C + W]
        gradient = own[...] * own_soft * (1.0 - own_soft)
        own[...] = gradient
        if step < ITERS - 1:
            copies_g = frames(own, gframe.at[step], HALO, OWN_R, g_send, g_recv)
            sends += copies_g

        squares = jnp.sum(gradient * gradient, axis=0, keepdims=True)
        squares = squares[:, :128] + squares[:, 128:]

        def reduce(value, at, slots, count, me, device):
            part[at] = value
            slots[step, pl.ds(me, 1)] = value[None]
            for k in range(1, count):
                pltpu.make_async_remote_copy(
                    part.at[at], slots.at[step, me], r_send.at[at], r_recv.at[at], device(k), MESH
                ).start()
            peers = slots.at[step, pl.ds(0, count - 1)]
            every = pltpu.make_async_remote_copy(
                peers, peers, r_send.at[at], r_recv.at[at], device(1), MESH
            )
            every.wait_recv()
            return jnp.sum(slots[step], axis=0), every

        stages = (
            (slots_c, 2, core, other_core),
            (slots_b, nb // 2, b // 2, same_core),
            (slots_w, nw, w, along_work),
        )
        for at, (slots, count, me, device) in enumerate(stages):
            squares, every = reduce(squares, 3 * step + at, slots, count, me, device)
            sends.append(every)
        mean = jnp.sum(squares, axis=1, keepdims=True) * (1.0 / (nb * nw * H * W))
        scale = STEP_SIZE / jnp.sqrt(mean + EPSILON)
        if step < ITERS - 1:
            for copy in copies_g:
                copy.wait_recv()
            frame[...] = frame[...] - scale * gframe[step]
        else:
            out_ref[...] = frame[OWN_R : OWN_R + H, OWN_C : OWN_C + W] - scale * gradient
    for copy in sends:
        copy.wait_send()


def solution(mesh):
    nb, nw = mesh.shape["band"], mesh.shape["work"]

    def shards(mask_logits, loss_weights, target_bits, kernels, kernel_gains, imager_list):
        by_col = jnp.transpose(kernels, (2, 0, 1))
        padded = jnp.pad(by_col, ((0, 1), (0, 0), (0, 7))).reshape(JP, K2, 4, 8)
        fwd = jnp.transpose(padded, (1, 2, 0, 3)).reshape(K2, KF)
        fwd = jnp.pad(fwd, ((0, 0), (0, KFP - KF)))
        flipped = jnp.pad(by_col[:, :, ::-1], ((0, 1), (0, 0), (0, 7))).reshape(JP, K2, 4, 8)
        bwd = jnp.transpose(flipped, (0, 2, 1, 3)).reshape(JP, KB)
        vmem = pl.BlockSpec(memory_space=pltpu.VMEM)
        smem = pl.BlockSpec(memory_space=pltpu.SMEM)
        dma = pltpu.SemaphoreType.DMA
        return pl.pallas_call(
            functools.partial(kernel, nb, nw),
            out_shape=jax.ShapeDtypeStruct((H, W), jnp.float32),
            in_specs=[vmem] * 5 + [smem] * 2,
            out_specs=vmem,
            scratch_shapes=[
                pltpu.VMEM((LR, LC), jnp.float32),
                pltpu.VMEM((ITERS, LR, LC), jnp.float32),
                pltpu.VMEM((H, W), jnp.bfloat16),
                pltpu.VMEM((H + 32, LC), jnp.bfloat16),
                pltpu.VMEM((ER, EC), jnp.float32),
                pltpu.VMEM((K2 * 8, KF), jnp.bfloat16),
                pltpu.VMEM((JP * 8, KB), jnp.bfloat16),
                pltpu.VMEM((LR // 8, JP * 8, EC), jnp.bfloat16),
                pltpu.VMEM((ER // 8, K2 * 8, EC), jnp.bfloat16),
                pltpu.VMEM((ITERS, 2, 1, 128), jnp.float32),
                pltpu.VMEM((ITERS, nb // 2, 1, 128), jnp.float32),
                pltpu.VMEM((ITERS, nw, 1, 128), jnp.float32),
                pltpu.VMEM((3 * ITERS, 1, 128), jnp.float32),
                dma((8,)), dma((8,)), dma((8,)), dma((8,)), dma((8,)), dma((8,)),
                dma((3 * ITERS,)), dma((3 * ITERS,)),
            ],
            compiler_params=pltpu.CompilerParams(
                collective_id=0, has_side_effects=True, vmem_limit_bytes=48 * 1024 * 1024
            ),
        )(
            mask_logits, loss_weights, target_bits, fwd, bwd, kernel_gains, imager_list.reshape(-1)
        )

    in_specs = (
        P("band", "work"),
        P("band", "work"),
        P("band", "work"),
        P(),
        P(),
        P("band", None, None, None),
    )
    return jax.shard_map(
        shards, mesh=mesh, in_specs=in_specs, out_specs=P("band", "work"), check_vma=False
    )
```

```python
import functools

import jax
import jax.numpy as jnp
from jax import lax
from jax.experimental import pallas as pl
from jax.experimental.pallas import tpu as pltpu
from jax.sharding import PartitionSpec as P

MESH = pl.DeviceIdType.MESH
TR = 24
H, W = 48, 256
K2 = 24
KS = 25
JP = 26
HALO = 24
ER, EC = 72, 384
LR, LC = 96, 512
OWN_R, OWN_C = 24, 128
KF = 4 * JP * 8
KFP = 896
KB = 4 * K2 * 8
ITERS = 2
STEEP, THRESH, STEP_SIZE, EPSILON = 4.0, 0.5, 0.5, 1e-6


def sigmoid(x):
    return 1.0 / (1.0 + jnp.exp(-x))


def kernel(
    nb, nw, log_ref, lw_ref, bits_ref, kf_ref, kb_ref, gain_ref, img_ref, out_ref,
    frame, gframe, vown, vframe, vext, tmat, umat, sblk, gblk, slots_c, slots_b, slots_w, part,
    a_send, a_recv, v_send, v_recv, g_send, g_recv, r_send, r_recv, knows_four, knows_all,
):
    b, w = lax.axis_index("band"), lax.axis_index("work")
    up, down = lax.rem(b + nb - 1, nb), lax.rem(b + 1, nb)
    left, right = lax.rem(w + nw - 1, nw), lax.rem(w + 1, nw)

    core = lax.rem(b, 2)

    def other_core(k):
        return (b + 1 - 2 * core, w)

    def same_core(k):
        return (lax.rem(b + 2 * k, nb), w)

    def along_work(k):
        return (b, lax.rem(w + k, nw))

    barrier = pltpu.get_barrier_semaphore()
    near = [along_work(k) for k in (1, 2, nw - 2, nw - 1)]
    far = [along_work(k) for k in (3, 4, nw - 4, nw - 3)]
    greeted = near + [same_core(k) for k in range(1, nb // 2)]
    greeted += [(up, w), (down, w), (up, left), (up, right), (down, left), (down, right)]
    for dev in greeted:
        pl.semaphore_signal(barrier, inc=1, device_id=dev, device_id_type=MESH)

    rows = lax.broadcasted_iota(jnp.int32, (H, W), 0)
    live0 = jnp.where(img_ref[w * 2] < nw, 1.0, 0.0)
    live1 = jnp.where(img_ref[w * 2 + 1] < nw, 1.0, 0.0)
    weight = lw_ref[...].astype(jnp.bfloat16).astype(jnp.float32)
    weight = weight * jnp.where(rows < TR, live0, live1)
    vown[...] = jnp.where(bits_ref[...] == 1, -weight, weight).astype(jnp.bfloat16)

    pl.semaphore_wait(barrier, len(greeted))
    for dev in near:
        pl.semaphore_signal(knows_four, inc=1, device_id=dev, device_id_type=MESH)

    def frames(src, dst, h, top, send, recv):
        lo, hi = slice(0, h), slice(H - h, H)
        first, last = slice(0, 128), slice(W - 128, W)
        above, below = slice(top - h, top), slice(top + H, top + H + h)
        mid = slice(top, top + H)
        before, after, centre = slice(0, 128), slice(128 + W, 256 + W), slice(128, 128 + W)
        plan = (
            (lo, slice(0, W), below, centre, (up, w)),
            (hi, slice(0, W), above, centre, (down, w)),
            (slice(0, H), first, mid, after, (b, left)),
            (slice(0, H), last, mid, before, (b, right)),
            (lo, first, below, after, (up, left)),
            (lo, last, below, before, (up, right)),
            (hi, first, above, after, (down, left)),
            (hi, last, above, before, (down, right)),
        )
        copies = []
        for k, (sr, sc, dr, dc, dev) in enumerate(plan):
            copies.append(
                pltpu.make_async_remote_copy(
                    src.at[sr, sc], dst.at[dr, dc], send.at[k], recv.at[k], dev, MESH
                )
            )
        for copy in copies:
            copy.start()
        return copies

    copies_v = frames(vown, vframe, 16, 16, v_send, v_recv)
    copies_a = frames(log_ref, frame, HALO, OWN_R, a_send, a_recv)
    frame[OWN_R : OWN_R + H, OWN_C : OWN_C + W] = log_ref[...]
    vframe[16 : 16 + H, 128 : 128 + W] = vown[...]

    lane_f = lax.broadcasted_iota(jnp.int32, (8, KFP), 1) & 7
    sub_f = lax.broadcasted_iota(jnp.int32, (8, KFP), 0)
    lane_b = lax.broadcasted_iota(jnp.int32, (8, KB), 1) & 7
    sub_b = lax.broadcasted_iota(jnp.int32, (8, KB), 0)

    def toeplitz(row, lane, sub, step):
        wide = jnp.broadcast_to(row.astype(jnp.float32), lane.shape)
        same = pltpu.roll(wide, 0, 1, stride=1, stride_axis=0)
        prior = pltpu.roll(wide, step - 8, 1, stride=1, stride_axis=0)
        return jnp.where(lane >= sub, same, prior)

    for c in range(0, K2, 2):
        pair = [toeplitz(kf_ref[c + d : c + d + 1, :], lane_f, sub_f, JP * 8) for d in range(2)]
        tmat[8 * c : 8 * c + 16, :] = jnp.concatenate(pair, axis=0)[:, :KF].astype(jnp.bfloat16)
    for j in range(0, JP, 2):
        pair = [toeplitz(kb_ref[j + d : j + d + 1, :], lane_b, sub_b, K2 * 8) for d in range(2)]
        umat[8 * j : 8 * j + 16, :] = jnp.concatenate(pair, axis=0).astype(jnp.bfloat16)

    for copy in copies_v:
        copy.wait_recv()
    band_row = b * H + lax.broadcasted_iota(jnp.int32, (ER, EC), 0) - 12
    band_col = w * W + lax.broadcasted_iota(jnp.int32, (ER, EC), 1) - 12
    inside = (band_row >= 0) & (band_row < nb * H) & (band_col >= 0) & (band_col < nw * W)
    signed = vframe[...].astype(jnp.float32)
    signed = pltpu.roll(signed, LC - 116, 1)[4 : 4 + ER, :EC]
    vext[...] = jnp.where(inside, signed, 0.0)

    for copy in copies_a:
        copy.wait_recv()
    pl.semaphore_wait(knows_four, len(near))
    for dev in far:
        pl.semaphore_signal(knows_all, inc=1, device_id=dev, device_id_type=MESH)

    band_row = b * H + lax.broadcasted_iota(jnp.int32, (LR, LC), 0) - OWN_R
    band_col = w * W + lax.broadcasted_iota(jnp.int32, (LR, LC), 1) - OWN_C
    inside = (band_row >= 0) & (band_row < nb * H) & (band_col >= 0) & (band_col < nw * W)

    sends = list(copies_v) + list(copies_a)
    for step in range(ITERS):
        soft = sigmoid(frame[...])
        own_soft = soft[OWN_R : OWN_R + H, OWN_C : OWN_C + W]
        mask = jnp.where(inside, soft.astype(jnp.bfloat16).astype(jnp.float32), 0.0)
        for j in range(0, JP, 2):
            pair = [
                pltpu.roll(mask, LC - 104 - min(j + d, KS - 1), 1)[:, :EC].reshape(LR // 8, 8, EC)
                for d in range(2)
            ]
            sblk[:, 8 * j : 8 * j + 16, :] = jnp.concatenate(pair, axis=1).astype(jnp.bfloat16)

        for blk in range(ER // 8):
            window = sblk[blk : blk + 4].reshape(KF, EC)
            fields = jnp.dot(tmat[...], window, preferred_element_type=jnp.float32)
            fields = fields.reshape(K2, 8, EC)
            intensity = jnp.zeros((8, EC), jnp.float32)
            for c in range(K2 // 2):
                f0, f1 = fields[c], fields[c + K2 // 2]
                intensity = intensity + gain_ref[c] * (f0 * f0 + f1 * f1)
            resist = sigmoid(STEEP * (intensity - THRESH))
            v = vext[8 * blk : 8 * blk + 8, :]
            target = jnp.where(v < 0.0, 1.0, 0.0)
            slopes = (8.0 * jnp.abs(v)) * (resist - target) * resist * (1.0 - resist)
            for c in range(0, K2, 2):
                pair = [2.0 * gain_ref[(c + d) % (K2 // 2)] * fields[c + d] * slopes for d in range(2)]
                gblk[blk, 8 * c : 8 * c + 16, :] = jnp.concatenate(pair, axis=0).astype(jnp.bfloat16)

        for blk in range(H // 8):
            window = gblk[blk : blk + 4].reshape(KB, EC)
            spread = jnp.dot(umat[...], window, preferred_element_type=jnp.float32)
            spread = spread.reshape(JP, 8, EC)
            total = jnp.zeros((8, W), jnp.float32)
            for j in range(KS):
                shift = (EC - (KS - 1 - j)) % EC
                total = total + pltpu.roll(spread[j], shift, 1)[:, :W]
            at = OWN_R + blk * 8
            gframe[step, at : at + 8, OWN_C : OWN_C + W] = total

        own = gframe.at[step, OWN_R : OWN_R + H, OWN_C : OWN_C + W]
        gradient = own[...] * own_soft * (1.0 - own_soft)
        own[...] = gradient
        if step < ITERS - 1:
            copies_g = frames(own, gframe.at[step], HALO, OWN_R, g_send, g_recv)
            sends += copies_g

        squares = jnp.sum(gradient * gradient, axis=0, keepdims=True)
        squares = squares[:, :128] + squares[:, 128:]

        def reduce(value, at, slots, count, me, device):
            part[at] = value
            slots[step, pl.ds(me, 1)] = value[None]
            for k in range(1, count):
                pltpu.make_async_remote_copy(
                    part.at[at], slots.at[step, me], r_send.at[at], r_recv.at[at], device(k), MESH
                ).start()
            peers = slots.at[step, pl.ds(0, count - 1)]
            every = pltpu.make_async_remote_copy(
                peers, peers, r_send.at[at], r_recv.at[at], device(1), MESH
            )
            every.wait_recv()
            return jnp.sum(slots[step], axis=0), every

        stages = (
            (slots_c, 2, core, other_core),
            (slots_b, nb // 2, b // 2, same_core),
            (slots_w, nw, w, along_work),
        )
        for at, (slots, count, me, device) in enumerate(stages):
            if step == 0 and at == len(stages) - 1:
                pl.semaphore_wait(knows_all, len(far))
            squares, every = reduce(squares, 3 * step + at, slots, count, me, device)
            sends.append(every)
        mean = jnp.sum(squares, axis=1, keepdims=True) * (1.0 / (nb * nw * H * W))
        scale = STEP_SIZE / jnp.sqrt(mean + EPSILON)
        if step < ITERS - 1:
            for copy in copies_g:
                copy.wait_recv()
            frame[...] = frame[...] - scale * gframe[step]
        else:
            out_ref[...] = frame[OWN_R : OWN_R + H, OWN_C : OWN_C + W] - scale * gradient
    for copy in sends:
        copy.wait_send()


def solution(mesh):
    nb, nw = mesh.shape["band"], mesh.shape["work"]

    def shards(mask_logits, loss_weights, target_bits, kernels, kernel_gains, imager_list):
        by_col = jnp.transpose(kernels, (2, 0, 1))
        padded = jnp.pad(by_col, ((0, 1), (0, 0), (0, 7))).reshape(JP, K2, 4, 8)
        fwd = jnp.transpose(padded, (1, 2, 0, 3)).reshape(K2, KF)
        fwd = jnp.pad(fwd, ((0, 0), (0, KFP - KF)))
        flipped = jnp.pad(by_col[:, :, ::-1], ((0, 1), (0, 0), (0, 7))).reshape(JP, K2, 4, 8)
        bwd = jnp.transpose(flipped, (0, 2, 1, 3)).reshape(JP, KB)
        vmem = pl.BlockSpec(memory_space=pltpu.VMEM)
        smem = pl.BlockSpec(memory_space=pltpu.SMEM)
        dma = pltpu.SemaphoreType.DMA
        return pl.pallas_call(
            functools.partial(kernel, nb, nw),
            out_shape=jax.ShapeDtypeStruct((H, W), jnp.float32),
            in_specs=[vmem] * 5 + [smem] * 2,
            out_specs=vmem,
            scratch_shapes=[
                pltpu.VMEM((LR, LC), jnp.float32),
                pltpu.VMEM((ITERS, LR, LC), jnp.float32),
                pltpu.VMEM((H, W), jnp.bfloat16),
                pltpu.VMEM((H + 32, LC), jnp.bfloat16),
                pltpu.VMEM((ER, EC), jnp.float32),
                pltpu.VMEM((K2 * 8, KF), jnp.bfloat16),
                pltpu.VMEM((JP * 8, KB), jnp.bfloat16),
                pltpu.VMEM((LR // 8, JP * 8, EC), jnp.bfloat16),
                pltpu.VMEM((ER // 8, K2 * 8, EC), jnp.bfloat16),
                pltpu.VMEM((ITERS, 2, 1, 128), jnp.float32),
                pltpu.VMEM((ITERS, nb // 2, 1, 128), jnp.float32),
                pltpu.VMEM((ITERS, nw, 1, 128), jnp.float32),
                pltpu.VMEM((3 * ITERS, 1, 128), jnp.float32),
                dma((8,)), dma((8,)), dma((8,)), dma((8,)), dma((8,)), dma((8,)),
                dma((3 * ITERS,)), dma((3 * ITERS,)),
                pltpu.SemaphoreType.REGULAR, pltpu.SemaphoreType.REGULAR,
            ],
            compiler_params=pltpu.CompilerParams(
                collective_id=0, has_side_effects=True, vmem_limit_bytes=48 * 1024 * 1024
            ),
        )(
            mask_logits, loss_weights, target_bits, fwd, bwd, kernel_gains, imager_list.reshape(-1)
        )

    in_specs = (
        P("band", "work"),
        P("band", "work"),
        P("band", "work"),
        P(),
        P(),
        P("band", None, None, None),
    )
    return jax.shard_map(
        shards, mesh=mesh, in_specs=in_specs, out_specs=P("band", "work"), check_vma=False
    )
```

```python
import functools

import jax
import jax.numpy as jnp
from jax import lax
from jax.experimental import pallas as pl
from jax.experimental.pallas import tpu as pltpu
from jax.sharding import PartitionSpec as P

MESH = pl.DeviceIdType.MESH
TR = 24
H, W = 48, 256
K2 = 24
KS = 25
JP = 26
HALO = 24
ER, EC = 72, 384
LR, LC = 96, 512
OWN_R, OWN_C = 24, 128
QF, QB = 256, 192
KF, KB = 4 * QF, 4 * QB
ITERS = 2
STEEP, THRESH, STEP_SIZE, EPSILON = 4.0, 0.5, 0.5, 1e-6


def sigmoid(x):
    return 1.0 / (1.0 + jnp.exp(-x))


def kernel(
    nb, nw, log_hbm, lw_hbm, bits_hbm, kern_hbm, gain_hbm, img_hbm, out_ref,
    log_ref, lw_ref, bits_ref, kern_ref, gain_ref, img_ref,
    frame, gframe, vown, vframe, vext, wide, tmat, umat, sblk, gblk,
    slots_c, slots_b, slots_w, part,
    l_sem, a_send, a_recv, v_send, v_recv, g_send, g_recv, r_send, r_recv, knows_four, knows_all,
):
    b, w = lax.axis_index("band"), lax.axis_index("work")
    up, down = lax.rem(b + nb - 1, nb), lax.rem(b + 1, nb)
    left, right = lax.rem(w + nw - 1, nw), lax.rem(w + 1, nw)

    core = lax.rem(b, 2)

    def other_core(k):
        return (b + 1 - 2 * core, w)

    def same_core(k):
        return (lax.rem(b + 2 * k, nb), w)

    def along_work(k):
        return (b, lax.rem(w + k, nw))

    barrier = pltpu.get_barrier_semaphore()
    near = [along_work(k) for k in (1, 2, nw - 2, nw - 1)]
    far = [along_work(k) for k in (3, 4, nw - 4, nw - 3)]
    greeted = near + [same_core(k) for k in range(1, nb // 2)]
    greeted += [(up, w), (down, w), (up, left), (up, right), (down, left), (down, right)]
    for dev in greeted:
        pl.semaphore_signal(barrier, inc=1, device_id=dev, device_id_type=MESH)

    pairs = (
        (lw_hbm, lw_ref), (bits_hbm, bits_ref), (img_hbm, img_ref),
        (log_hbm, log_ref), (kern_hbm, kern_ref), (gain_hbm, gain_ref),
    )
    loads = [pltpu.make_async_copy(src, dst, l_sem.at[k]) for k, (src, dst) in enumerate(pairs)]
    for load in loads:
        load.start()
    sblk[:, 8 * JP :, :] = jnp.zeros((LR // 8, QF - 8 * JP, EC), jnp.bfloat16)
    for load in loads[:3]:
        load.wait()

    rows = lax.broadcasted_iota(jnp.int32, (H, W), 0)
    live0 = jnp.where(img_ref[0, 0, 0, w] < nw, 1.0, 0.0)
    live1 = jnp.where(img_ref[0, 1, 0, w] < nw, 1.0, 0.0)
    weight = lw_ref[...].astype(jnp.bfloat16).astype(jnp.float32)
    weight = weight * jnp.where(rows < TR, live0, live1)
    vown[...] = jnp.where(bits_ref[...] == 1, -weight, weight).astype(jnp.bfloat16)

    pl.semaphore_wait(barrier, len(greeted))
    for dev in near:
        pl.semaphore_signal(knows_four, inc=1, device_id=dev, device_id_type=MESH)

    def frames(src, dst, h, top, send, recv):
        lo, hi = slice(0, h), slice(H - h, H)
        first, last = slice(0, 128), slice(W - 128, W)
        above, below = slice(top - h, top), slice(top + H, top + H + h)
        mid = slice(top, top + H)
        before, after, centre = slice(0, 128), slice(128 + W, 256 + W), slice(128, 128 + W)
        plan = (
            (lo, slice(0, W), below, centre, (up, w)),
            (hi, slice(0, W), above, centre, (down, w)),
            (slice(0, H), first, mid, after, (b, left)),
            (slice(0, H), last, mid, before, (b, right)),
            (lo, first, below, after, (up, left)),
            (lo, last, below, before, (up, right)),
            (hi, first, above, after, (down, left)),
            (hi, last, above, before, (down, right)),
        )
        copies = []
        for k, (sr, sc, dr, dc, dev) in enumerate(plan):
            copies.append(
                pltpu.make_async_remote_copy(
                    src.at[sr, sc], dst.at[dr, dc], send.at[k], recv.at[k], dev, MESH
                )
            )
        for copy in copies:
            copy.start()
        return copies

    loads[3].wait()
    copies_v = frames(vown, vframe, 16, 16, v_send, v_recv)
    copies_a = frames(log_ref, frame, HALO, OWN_R, a_send, a_recv)
    frame[OWN_R : OWN_R + H, OWN_C : OWN_C + W] = log_ref[...]
    vframe[16 : 16 + H, 128 : 128 + W] = vown[...]

    for load in loads[4:]:
        load.wait()
    taps = jnp.transpose(kern_ref[...].astype(jnp.float32).reshape(KS * K2, KS)).astype(jnp.bfloat16)
    lane = lax.broadcasted_iota(jnp.int32, (1, KF), 1)
    channel = (lane >> 3) & 31
    tap = KS - 1 - 8 * (lane >> 8) - (lane & 7)
    source = jnp.where((channel < K2) & (tap >= 0), tap * K2 + channel, -1)
    chosen = lax.broadcasted_iota(jnp.int32, (KS * K2, KF), 0) == source
    chosen = jnp.where(chosen, 1.0, 0.0).astype(jnp.bfloat16)
    base = jnp.dot(taps, chosen, preferred_element_type=jnp.float32)
    lane8 = lax.broadcasted_iota(jnp.int32, (8, KF), 1) & 7
    sub = lax.broadcasted_iota(jnp.int32, (8, KF), 0)
    for j in range(KS):
        row = jnp.broadcast_to(base[j : j + 1, :], (8, KF))
        same = pltpu.roll(row, 0, 1, stride=1, stride_axis=0)
        prior = pltpu.roll(row, QF - 8, 1, stride=1, stride_axis=0)
        wide[8 * j : 8 * j + 8, :] = jnp.where(lane8 >= sub, same, prior)
    wide[8 * KS :, :] = jnp.zeros((QF - 8 * KS, KF), jnp.float32)
    for q in range(4):
        umat[:, QB * q : QB * q + QB] = wide[: 8 * JP, QF * q : QF * q + QB].astype(jnp.bfloat16)
        turned = jnp.transpose(wide[:, QF * (3 - q) : QF * (4 - q)])
        tmat[:, QF * q : QF * q + QF] = turned[:QB].astype(jnp.bfloat16)

    for copy in copies_v:
        copy.wait_recv()
    band_row = b * H + lax.broadcasted_iota(jnp.int32, (ER, EC), 0) - 12
    band_col = w * W + lax.broadcasted_iota(jnp.int32, (ER, EC), 1) - 12
    inside = (band_row >= 0) & (band_row < nb * H) & (band_col >= 0) & (band_col < nw * W)
    signed = vframe[...].astype(jnp.float32)
    signed = pltpu.roll(signed, LC - 116, 1)[4 : 4 + ER, :EC]
    vext[...] = jnp.where(inside, signed, 0.0)

    for copy in copies_a:
        copy.wait_recv()
    pl.semaphore_wait(knows_four, len(near))
    for dev in far:
        pl.semaphore_signal(knows_all, inc=1, device_id=dev, device_id_type=MESH)

    band_row = b * H + lax.broadcasted_iota(jnp.int32, (LR, LC), 0) - OWN_R
    band_col = w * W + lax.broadcasted_iota(jnp.int32, (LR, LC), 1) - OWN_C
    inside = (band_row >= 0) & (band_row < nb * H) & (band_col >= 0) & (band_col < nw * W)

    sends = list(copies_v) + list(copies_a)
    for step in range(ITERS):
        soft = sigmoid(frame[...])
        own_soft = soft[OWN_R : OWN_R + H, OWN_C : OWN_C + W]
        mask = jnp.where(inside, soft.astype(jnp.bfloat16).astype(jnp.float32), 0.0)
        for j in range(0, JP, 2):
            pair = [
                pltpu.roll(mask, LC - 104 - min(j + d, KS - 1), 1)[:, :EC].reshape(LR // 8, 8, EC)
                for d in range(2)
            ]
            sblk[:, 8 * j : 8 * j + 16, :] = jnp.concatenate(pair, axis=1).astype(jnp.bfloat16)

        for blk in range(ER // 8):
            window = sblk[blk : blk + 4].reshape(KF, EC)
            fields = jnp.dot(tmat[...], window, preferred_element_type=jnp.float32)
            fields = fields.reshape(K2, 8, EC)
            intensity = jnp.zeros((8, EC), jnp.float32)
            for c in range(K2 // 2):
                f0, f1 = fields[c], fields[c + K2 // 2]
                intensity = intensity + gain_ref[c] * (f0 * f0 + f1 * f1)
            resist = sigmoid(STEEP * (intensity - THRESH))
            v = vext[8 * blk : 8 * blk + 8, :]
            target = jnp.where(v < 0.0, 1.0, 0.0)
            slopes = (8.0 * jnp.abs(v)) * (resist - target) * resist * (1.0 - resist)
            for c in range(0, K2, 2):
                pair = [2.0 * gain_ref[(c + d) % (K2 // 2)] * fields[c + d] * slopes for d in range(2)]
                gblk[blk, 8 * c : 8 * c + 16, :] = jnp.concatenate(pair, axis=0).astype(jnp.bfloat16)

        for blk in range(H // 8):
            window = gblk[blk : blk + 4].reshape(KB, EC)
            spread = jnp.dot(umat[...], window, preferred_element_type=jnp.float32)
            spread = spread.reshape(JP, 8, EC)
            total = jnp.zeros((8, W), jnp.float32)
            for j in range(KS):
                shift = (EC - (KS - 1 - j)) % EC
                total = total + pltpu.roll(spread[j], shift, 1)[:, :W]
            at = OWN_R + blk * 8
            gframe[step, at : at + 8, OWN_C : OWN_C + W] = total

        own = gframe.at[step, OWN_R : OWN_R + H, OWN_C : OWN_C + W]
        gradient = own[...] * own_soft * (1.0 - own_soft)
        own[...] = gradient
        if step < ITERS - 1:
            copies_g = frames(own, gframe.at[step], HALO, OWN_R, g_send, g_recv)
            sends += copies_g

        squares = jnp.sum(gradient * gradient, axis=0, keepdims=True)
        squares = squares[:, :128] + squares[:, 128:]

        def reduce(value, at, slots, count, me, device):
            part[at] = value
            slots[step, pl.ds(me, 1)] = value[None]
            for k in range(1, count):
                pltpu.make_async_remote_copy(
                    part.at[at], slots.at[step, me], r_send.at[at], r_recv.at[at], device(k), MESH
                ).start()
            peers = slots.at[step, pl.ds(0, count - 1)]
            every = pltpu.make_async_remote_copy(
                peers, peers, r_send.at[at], r_recv.at[at], device(1), MESH
            )
            every.wait_recv()
            return jnp.sum(slots[step], axis=0), every

        stages = (
            (slots_c, 2, core, other_core),
            (slots_b, nb // 2, b // 2, same_core),
            (slots_w, nw, w, along_work),
        )
        for at, (slots, count, me, device) in enumerate(stages):
            if step == 0 and at == len(stages) - 1:
                pl.semaphore_wait(knows_all, len(far))
            squares, every = reduce(squares, 3 * step + at, slots, count, me, device)
            sends.append(every)
        mean = jnp.sum(squares, axis=1, keepdims=True) * (1.0 / (nb * nw * H * W))
        scale = STEP_SIZE / jnp.sqrt(mean + EPSILON)
        if step < ITERS - 1:
            for copy in copies_g:
                copy.wait_recv()
            frame[...] = frame[...] - scale * gframe[step]
        else:
            out_ref[...] = frame[OWN_R : OWN_R + H, OWN_C : OWN_C + W] - scale * gradient
    for copy in sends:
        copy.wait_send()


def solution(mesh):
    nb, nw = mesh.shape["band"], mesh.shape["work"]

    def shards(mask_logits, loss_weights, target_bits, kernels, kernel_gains, imager_list):
        vmem = pl.BlockSpec(memory_space=pltpu.VMEM)
        hbm = pl.BlockSpec(memory_space=pltpu.HBM)
        dma = pltpu.SemaphoreType.DMA
        return pl.pallas_call(
            functools.partial(kernel, nb, nw),
            out_shape=jax.ShapeDtypeStruct((H, W), jnp.float32),
            in_specs=[hbm] * 6,
            out_specs=vmem,
            scratch_shapes=[
                pltpu.VMEM((H, W), jnp.float32),
                pltpu.VMEM((H, W), jnp.float32),
                pltpu.VMEM((H, W), jnp.int32),
                pltpu.VMEM((KS, K2, KS), jnp.bfloat16),
                pltpu.SMEM((K2 // 2,), jnp.float32),
                pltpu.SMEM((1, H // TR, 1, nw), jnp.int32),
                pltpu.VMEM((LR, LC), jnp.float32),
                pltpu.VMEM((ITERS, LR, LC), jnp.float32),
                pltpu.VMEM((H, W), jnp.bfloat16),
                pltpu.VMEM((H + 32, LC), jnp.bfloat16),
                pltpu.VMEM((ER, EC), jnp.float32),
                pltpu.VMEM((QF, KF), jnp.float32),
                pltpu.VMEM((QB, KF), jnp.bfloat16),
                pltpu.VMEM((JP * 8, KB), jnp.bfloat16),
                pltpu.VMEM((LR // 8, QF, EC), jnp.bfloat16),
                pltpu.VMEM((ER // 8, QB, EC), jnp.bfloat16),
                pltpu.VMEM((ITERS, 2, 1, 128), jnp.float32),
                pltpu.VMEM((ITERS, nb // 2, 1, 128), jnp.float32),
                pltpu.VMEM((ITERS, nw, 1, 128), jnp.float32),
                pltpu.VMEM((3 * ITERS, 1, 128), jnp.float32),
                dma((6,)), dma((8,)), dma((8,)), dma((8,)), dma((8,)), dma((8,)), dma((8,)),
                dma((3 * ITERS,)), dma((3 * ITERS,)),
                pltpu.SemaphoreType.REGULAR, pltpu.SemaphoreType.REGULAR,
            ],
            compiler_params=pltpu.CompilerParams(
                collective_id=0, has_side_effects=True, vmem_limit_bytes=62 * 1024 * 1024
            ),
        )(
            mask_logits,
            loss_weights,
            target_bits,
            jnp.transpose(kernels, (1, 0, 2)),
            kernel_gains,
            jnp.transpose(imager_list, (0, 2, 3, 1)),
        )

    in_specs = (
        P("band", "work"),
        P("band", "work"),
        P("band", "work"),
        P(),
        P(),
        P("band", None, None, None),
    )
    return jax.shard_map(
        shards, mesh=mesh, in_specs=in_specs, out_specs=P("band", "work"), check_vma=False
    )
```

```python
import functools

import jax
import jax.numpy as jnp
from jax import lax
from jax.experimental import pallas as pl
from jax.experimental.pallas import tpu as pltpu
from jax.sharding import PartitionSpec as P

MESH = pl.DeviceIdType.MESH
TR = 24
H, W = 48, 256
K2 = 24
KS = 25
JP = 26
HALO = 24
ER, EC = 72, 256
XC = 24
SLOT, XL, XG = 48, 512, 384
XAT = 104 + EC
LR, LC = 96, 512
OWN_R, OWN_C = 24, 128
QF, QB = 256, 192
KF, KB = 4 * QF, 4 * QB
ITERS = 2
STEEP, THRESH, STEP_SIZE, EPSILON = 4.0, 0.5, 0.5, 1e-6


def farthest_first(*rings):
    count = 1
    for ring in rings:
        count *= ring

    def links(k):
        total = 0
        for ring in reversed(rings):
            total += min(k % ring, ring - k % ring)
            k //= ring
        return total

    return sorted(range(1, count), key=lambda k: -links(k))


def sigmoid(x):
    return 1.0 / (1.0 + jnp.exp(-x))


def kernel(
    nb, nw, log_hbm, lw_hbm, bits_hbm, kern_hbm, gain_hbm, img_hbm, out_ref,
    lw_ref, bits_ref, kern_ref, gain_ref, img_ref,
    both, frame, gframe, vext, vlast, mlast, wide, tmat, umat, sblk, sxblk, gblk, gxblk,
    slots_c, slots_b, slots_w, part,
    l_sem, a_send, a_recv, g_send, g_recv, r_send, r_recv, knows_four, knows_all,
):
    b, w = lax.axis_index("band"), lax.axis_index("work")
    up, down = lax.rem(b + nb - 1, nb), lax.rem(b + 1, nb)
    left, right = lax.rem(w + nw - 1, nw), lax.rem(w + 1, nw)

    core = lax.rem(b, 2)

    def other_core(k):
        return (b + 1 - 2 * core, w)

    def same_core(k):
        return (lax.rem(b + 2 * k, nb), w)

    def along_work(k):
        return (b, lax.rem(w + k, nw))

    barrier = pltpu.get_barrier_semaphore()
    near = [along_work(k) for k in (1, 2, nw - 2, nw - 1)]
    far = [along_work(k) for k in (3, 4, nw - 4, nw - 3)]
    greeted = [(up, left), (up, right), (down, left), (down, right), (up, w), (down, w)]
    greeted += near + [same_core(k) for k in range(1, nb // 2)]
    for dev in greeted:
        pl.semaphore_signal(barrier, inc=1, device_id=dev, device_id_type=MESH)

    pairs = (
        (lw_hbm, lw_ref), (bits_hbm, bits_ref), (img_hbm, img_ref),
        (log_hbm, both.at[0]), (kern_hbm, kern_ref), (gain_hbm, gain_ref),
    )
    loads = [pltpu.make_async_copy(src, dst, l_sem.at[k]) for k, (src, dst) in enumerate(pairs)]
    for load in loads:
        load.start()
    sblk[:, 8 * JP :, :] = jnp.zeros((LR // 8, QF - 8 * JP, EC), jnp.bfloat16)
    for q in range(4):
        sxblk[QF * q + 8 * JP : QF * q + QF, :] = jnp.zeros((QF - 8 * JP, XL), jnp.bfloat16)
    for load in loads[:3]:
        load.wait()

    rows = lax.broadcasted_iota(jnp.int32, (H, W), 0)
    live0 = jnp.where(img_ref[0, 0, 0, w] < nw, 1.0, 0.0)
    live1 = jnp.where(img_ref[0, 1, 0, w] < nw, 1.0, 0.0)
    weight = lw_ref[...].astype(jnp.bfloat16).astype(jnp.float32)
    weight = weight * jnp.where(rows < TR, live0, live1)
    both[1] = jnp.where(bits_ref[...] == 1, -weight, weight)

    pl.semaphore_wait(barrier, len(greeted))
    for dev in near:
        pl.semaphore_signal(knows_four, inc=1, device_id=dev, device_id_type=MESH)

    def rims(src, dst, send, recv):
        every = slice(None)
        lo, hi = slice(0, HALO), slice(H - HALO, H)
        first, last = slice(0, 128), slice(W - 128, W)
        above, below, mid = slice(0, OWN_R), slice(OWN_R + H, LR), slice(OWN_R, OWN_R + H)
        before, after, centre = slice(0, OWN_C), slice(OWN_C + W, LC), slice(OWN_C, OWN_C + W)
        plan = (
            (lo, first, below, after, (up, left)),
            (lo, last, below, before, (up, right)),
            (hi, first, above, after, (down, left)),
            (hi, last, above, before, (down, right)),
            (lo, slice(0, W), below, centre, (up, w)),
            (hi, slice(0, W), above, centre, (down, w)),
            (slice(0, H), first, mid, after, (b, left)),
            (slice(0, H), last, mid, before, (b, right)),
        )
        copies = []
        for k, (sr, sc, dr, dc, dev) in enumerate(plan):
            copies.append(
                pltpu.make_async_remote_copy(
                    src.at[every, sr, sc], dst.at[every, dr, dc], send.at[k], recv.at[k], dev, MESH
                )
            )
        for copy in copies:
            copy.start()
        return copies

    loads[3].wait()
    copies_a = rims(both, frame, a_send, a_recv)
    frame[:, OWN_R : OWN_R + H, OWN_C : OWN_C + W] = both[...]

    for load in loads[4:]:
        load.wait()
    taps = jnp.transpose(kern_ref[...].astype(jnp.float32).reshape(KS * K2, KS)).astype(jnp.bfloat16)
    lane = lax.broadcasted_iota(jnp.int32, (1, KF), 1)
    channel = (lane >> 3) & 31
    tap = KS - 1 - 8 * (lane >> 8) - (lane & 7)
    source = jnp.where((channel < K2) & (tap >= 0), tap * K2 + channel, -1)
    chosen = lax.broadcasted_iota(jnp.int32, (KS * K2, KF), 0) == source
    chosen = jnp.where(chosen, 1.0, 0.0).astype(jnp.bfloat16)
    base = jnp.dot(taps, chosen, preferred_element_type=jnp.float32)
    lane8 = lax.broadcasted_iota(jnp.int32, (8, KF), 1) & 7
    sub = lax.broadcasted_iota(jnp.int32, (8, KF), 0)
    for j in range(KS):
        row = jnp.broadcast_to(base[j : j + 1, :], (8, KF))
        same = pltpu.roll(row, 0, 1, stride=1, stride_axis=0)
        prior = pltpu.roll(row, QF - 8, 1, stride=1, stride_axis=0)
        wide[8 * j : 8 * j + 8, :] = jnp.where(lane8 >= sub, same, prior)
    wide[8 * KS :, :] = jnp.zeros((QF - 8 * KS, KF), jnp.float32)
    for q in range(4):
        umat[:, QB * q : QB * q + QB] = wide[: 8 * JP, QF * q : QF * q + QB].astype(jnp.bfloat16)
        turned = jnp.transpose(wide[:, QF * (3 - q) : QF * (4 - q)])
        tmat[:, QF * q : QF * q + QF] = turned[:QB].astype(jnp.bfloat16)

    def weights(low, high):
        shape = (high - low, LC)
        band_row = b * H + lax.broadcasted_iota(jnp.int32, shape, 0) + (low - 12)
        band_col = w * W + lax.broadcasted_iota(jnp.int32, shape, 1) - OWN_C
        inside = (band_row >= 0) & (band_row < nb * H) & (band_col >= 0) & (band_col < nw * W)
        signed = jnp.where(inside, frame[1, 12 + low : 12 + high, :], 0.0)
        signed = pltpu.roll(signed, LC - 116, 1)
        vext[low:high, :] = signed[:, :EC]
        vlast[low:high, :] = jnp.where(slot_lane[:, :128] < XC, signed[:, EC : EC + 128], 0.0)

    slot_lane = lax.broadcasted_iota(jnp.int32, (1, LC), 1)
    band_col = w * W + lax.broadcasted_iota(jnp.int32, (8, LC), 1) - OWN_C
    middle = jnp.where((band_col >= 0) & (band_col < nw * W), 1.0, 0.0)
    upper, lower = jnp.where(b > 0, middle, 0.0), jnp.where(b < nb - 1, middle, 0.0)

    sends = list(copies_a)
    for step in range(ITERS):
        def shifted(blk):
            inside = upper if blk < 3 else middle if blk < 9 else lower
            soft = sigmoid(frame[0, 8 * blk : 8 * blk + 8, :])
            rows8 = soft.astype(jnp.bfloat16).astype(jnp.float32) * inside
            last = pltpu.roll(rows8, LC - XAT, 1)[:, :128]
            mlast[8 * blk : 8 * blk + 8, :] = jnp.where(slot_lane[:, :128] < SLOT, last, 0.0)
            rows8 = rows8[:, :XG]
            for j in range(0, JP, 2):
                pair = [pltpu.roll(rows8, XG - 104 - min(j + d, KS - 1), 1)[:, :EC] for d in range(2)]
                sblk[blk, 8 * j : 8 * j + 16, :] = jnp.concatenate(pair, axis=0).astype(jnp.bfloat16)

        def side_by_side(ref, height):
            total = None
            for blk in range(ER // 8):
                part = ref[8 * blk : 8 * blk + height, :]
                part = jnp.concatenate([part, jnp.zeros((height, XL - 128), jnp.float32)], axis=1)
                part = pltpu.roll(part, SLOT * blk, 1) if blk else part
                total = part if total is None else total + part
            return total

        def shifted_last():
            rows32 = side_by_side(mlast, 32)
            for j in range(0, JP, 2):
                pair = []
                for d in range(2):
                    shift = min(j + d, KS - 1)
                    pair.append(pltpu.roll(rows32, XL - shift, 1) if shift else rows32)
                for q in range(4):
                    both8 = [p[8 * q : 8 * q + 8] for p in pair]
                    at = QF * q + 8 * j
                    sxblk[at : at + 16, :] = jnp.concatenate(both8, axis=0).astype(jnp.bfloat16)

        def field_gradient(fields, v, store):
            lanes = v.shape[1]
            fields = fields.reshape(K2, 8, lanes)
            intensity = jnp.zeros((8, lanes), jnp.float32)
            for c in range(K2 // 2):
                f0, f1 = fields[c], fields[c + K2 // 2]
                intensity = intensity + gain_ref[c] * (f0 * f0 + f1 * f1)
            resist = sigmoid(STEEP * (intensity - THRESH))
            target = jnp.where(v < 0.0, 1.0, 0.0)
            slopes = (8.0 * jnp.abs(v)) * (resist - target) * resist * (1.0 - resist)
            for c in range(0, K2, 2):
                pair = [2.0 * gain_ref[(c + d) % (K2 // 2)] * fields[c + d] * slopes for d in range(2)]
                store(8 * c, jnp.concatenate(pair, axis=0))

        def forward(blk):
            window = sblk[blk : blk + 4].reshape(KF, EC)
            fields = jnp.dot(tmat[...], window, preferred_element_type=jnp.float32)

            def store(at, value):
                gblk[blk, at : at + 16, :] = value.astype(jnp.bfloat16)

            field_gradient(fields, vext[8 * blk : 8 * blk + 8, :], store)

        def forward_last():
            fields = jnp.dot(tmat[...], sxblk[...], preferred_element_type=jnp.float32)

            def store(at, value):
                for q in range(4):
                    moved = pltpu.roll(value, XL - SLOT * q, 1) if q else value
                    if XL - SLOT * q < XG:
                        moved = jnp.where(slot_lane < XL - SLOT * q, moved, 0.0)
                    gxblk[QB * q + at : QB * q + at + 16, :] = moved[:, :XG].astype(jnp.bfloat16)

            field_gradient(fields, side_by_side(vlast, 8), store)

        def backward_last():
            spread = jnp.dot(umat[...], gxblk[...], preferred_element_type=jnp.float32)
            spread = spread.reshape(JP, 8, XG)
            total = spread[0]
            for j in range(1, KS):
                total = total + pltpu.roll(spread[j], j, 1)
            lane = lax.broadcasted_iota(jnp.int32, (8, W), 1)
            parts = [pltpu.roll(total, (W - XC - SLOT * k) % XG, 1)[:, :W] for k in range(H // 8)]
            return jnp.concatenate([jnp.where(lane >= W - XC, p, 0.0) for p in parts], axis=0)

        def backward(blk):
            window = gblk[blk : blk + 4].reshape(KB, EC)
            spread = jnp.dot(umat[...], window, preferred_element_type=jnp.float32)
            spread = spread.reshape(JP, 8, EC)
            lane = lax.broadcasted_iota(jnp.int32, (8, EC), 1)
            total = jnp.zeros((8, W), jnp.float32)
            for j in range(KS):
                shift = KS - 1 - j
                moved = pltpu.roll(spread[j], EC - shift, 1) if shift else spread[j]
                total = total + jnp.where(lane < W - shift, moved, 0.0)
            at = OWN_R + blk * 8
            gframe[step, at : at + 8, OWN_C : OWN_C + W] = total

        if step == 0:
            for copy in copies_a[6:]:
                copy.wait_recv()
            weights(24, 48)
        for blk in range(3, 9):
            shifted(blk)
        for blk in range(3, 6):
            forward(blk)
        if step == 0:
            for copy in copies_a[:6]:
                copy.wait_recv()
            pl.semaphore_wait(knows_four, len(near))
            for dev in far:
                pl.semaphore_signal(knows_all, inc=1, device_id=dev, device_id_type=MESH)
            weights(0, 24)
            weights(48, 72)
        for blk in (0, 1, 2):
            shifted(blk)
        for blk in (0, 1, 2):
            forward(blk)
        for blk in (9, 10, 11):
            shifted(blk)
        shifted_last()
        forward_last()
        for blk in (6, 7, 8):
            forward(blk)
        for blk in (0, 1, 2):
            backward(blk)
        last = backward_last()
        for blk in (3, 4, 5):
            backward(blk)

        own = gframe.at[step, OWN_R : OWN_R + H, OWN_C : OWN_C + W]
        own_soft = sigmoid(frame[0, OWN_R : OWN_R + H, OWN_C : OWN_C + W])
        gradient = (own[...] + last) * own_soft * (1.0 - own_soft)
        own[...] = gradient
        if step < ITERS - 1:
            copies_g = rims(gframe.at[pl.ds(step, 1), OWN_R : OWN_R + H, OWN_C : OWN_C + W], gframe.at[pl.ds(step, 1)], g_send, g_recv)
            sends += copies_g

        squares = jnp.sum(gradient * gradient, axis=0, keepdims=True)
        squares = squares[:, :128] + squares[:, 128:]

        def reduce(value, at, slots, order, me, device):
            count = len(order) + 1
            part[at] = value
            slots[step, pl.ds(me, 1)] = value[None]
            for k in order:
                pltpu.make_async_remote_copy(
                    part.at[at], slots.at[step, me], r_send.at[at], r_recv.at[at], device(k), MESH
                ).start()
            peers = slots.at[step, pl.ds(0, count - 1)]
            every = pltpu.make_async_remote_copy(
                peers, peers, r_send.at[at], r_recv.at[at], device(1), MESH
            )
            every.wait_recv()
            return jnp.sum(slots[step], axis=0), every

        stages = (
            (slots_c, [1], core, other_core),
            (slots_b, farthest_first(nb // 8, 4), b // 2, same_core),
            (slots_w, farthest_first(nw), w, along_work),
        )
        for at, (slots, order, me, device) in enumerate(stages):
            if step == 0 and at == len(stages) - 1:
                pl.semaphore_wait(knows_all, len(far))
            squares, every = reduce(squares, 3 * step + at, slots, order, me, device)
            sends.append(every)
        mean = jnp.sum(squares, axis=1, keepdims=True) * (1.0 / (nb * nw * H * W))
        scale = STEP_SIZE / jnp.sqrt(mean + EPSILON)
        if step < ITERS - 1:
            for copy in copies_g:
                copy.wait_recv()
            frame[0] = frame[0] - scale * gframe[step]
        else:
            out_ref[...] = frame[0, OWN_R : OWN_R + H, OWN_C : OWN_C + W] - scale * gradient
    for copy in sends:
        copy.wait_send()


def solution(mesh):
    nb, nw = mesh.shape["band"], mesh.shape["work"]

    def shards(mask_logits, loss_weights, target_bits, kernels, kernel_gains, imager_list):
        vmem = pl.BlockSpec(memory_space=pltpu.VMEM)
        hbm = pl.BlockSpec(memory_space=pltpu.HBM)
        dma = pltpu.SemaphoreType.DMA
        return pl.pallas_call(
            functools.partial(kernel, nb, nw),
            out_shape=jax.ShapeDtypeStruct((H, W), jnp.float32),
            in_specs=[hbm] * 6,
            out_specs=vmem,
            scratch_shapes=[
                pltpu.VMEM((H, W), jnp.float32),
                pltpu.VMEM((H, W), jnp.int32),
                pltpu.VMEM((KS, K2, KS), jnp.bfloat16),
                pltpu.SMEM((K2 // 2,), jnp.float32),
                pltpu.SMEM((1, H // TR, 1, nw), jnp.int32),
                pltpu.VMEM((2, H, W), jnp.float32),
                pltpu.VMEM((2, LR, LC), jnp.float32),
                pltpu.VMEM((ITERS, LR, LC), jnp.float32),
                pltpu.VMEM((ER, EC), jnp.float32),
                pltpu.VMEM((ER, 128), jnp.float32),
                pltpu.VMEM((LR, 128), jnp.float32),
                pltpu.VMEM((QF, KF), jnp.float32),
                pltpu.VMEM((QB, KF), jnp.bfloat16),
                pltpu.VMEM((JP * 8, KB), jnp.bfloat16),
                pltpu.VMEM((LR // 8, QF, EC), jnp.bfloat16),
                pltpu.VMEM((KF, XL), jnp.bfloat16),
                pltpu.VMEM((ER // 8, QB, EC), jnp.bfloat16),
                pltpu.VMEM((KB, XG), jnp.bfloat16),
                pltpu.VMEM((ITERS, 2, 1, 128), jnp.float32),
                pltpu.VMEM((ITERS, nb // 2, 1, 128), jnp.float32),
                pltpu.VMEM((ITERS, nw, 1, 128), jnp.float32),
                pltpu.VMEM((3 * ITERS, 1, 128), jnp.float32),
                dma((6,)), dma((8,)), dma((8,)), dma((8,)), dma((8,)),
                dma((3 * ITERS,)), dma((3 * ITERS,)),
                pltpu.SemaphoreType.REGULAR, pltpu.SemaphoreType.REGULAR,
            ],
            compiler_params=pltpu.CompilerParams(
                collective_id=0, has_side_effects=True, vmem_limit_bytes=62 * 1024 * 1024
            ),
        )(
            mask_logits,
            loss_weights,
            target_bits,
            jnp.transpose(kernels, (1, 0, 2)),
            kernel_gains,
            jnp.transpose(imager_list, (0, 2, 3, 1)),
        )

    in_specs = (
        P("band", "work"),
        P("band", "work"),
        P("band", "work"),
        P(),
        P(),
        P("band", None, None, None),
    )
    return jax.shard_map(
        shards, mesh=mesh, in_specs=in_specs, out_specs=P("band", "work"), check_vma=False
    )
```

```python
import functools

import jax
import jax.numpy as jnp
from jax import lax
from jax.experimental import pallas as pl
from jax.experimental.pallas import tpu as pltpu
from jax.sharding import PartitionSpec as P

MESH = pl.DeviceIdType.MESH
TR = 24
H, W = 48, 256
K2 = 24
KS = 25
JP = 26
HALO = 24
ER, EC = 72, 256
XC = 24
SLOT, XL, XG = 48, 512, 384
XAT = 104 + EC
LR, LC = 96, 512
OWN_R, OWN_C = 24, 128
QF, QB = 256, 192
KF, KB = 4 * QF, 4 * QB
ITERS = 2
STEEP, THRESH, STEP_SIZE, EPSILON = 4.0, 0.5, 0.5, 1e-6


def farthest_first(*rings):
    count = 1
    for ring in rings:
        count *= ring

    def links(k):
        total = 0
        for ring in reversed(rings):
            total += min(k % ring, ring - k % ring)
            k //= ring
        return total

    return sorted(range(1, count), key=lambda k: -links(k))


def sigmoid(x):
    return 1.0 / (1.0 + jnp.exp(-x))


def kernel(
    nb, nw, log_hbm, lw_hbm, bits_hbm, kern_hbm, gain_hbm, img_hbm, out_ref,
    lw_ref, bits_ref, kern_ref, gain_ref, img_ref,
    both, frame, gframe, vext, vlast, mlast, wide, tmat, umat, sblk, sxblk, gblk, gxblk,
    slots_c, slots_b, slots_w, part,
    l_sem, a_send, a_recv, g_send, g_recv, r_send, r_recv, knows_four, knows_all,
):
    b, w = lax.axis_index("band"), lax.axis_index("work")
    up, down = lax.rem(b + nb - 1, nb), lax.rem(b + 1, nb)
    left, right = lax.rem(w + nw - 1, nw), lax.rem(w + 1, nw)

    core = lax.rem(b, 2)

    def other_core(k):
        return (b + 1 - 2 * core, w)

    def same_core(k):
        return (lax.rem(b + 2 * k, nb), w)

    def along_work(k):
        return (b, lax.rem(w + k, nw))

    barrier = pltpu.get_barrier_semaphore()
    near = [along_work(k) for k in (1, 2, nw - 2, nw - 1)]
    far = [along_work(k) for k in (3, 4, nw - 4, nw - 3)]
    greeted = [(up, left), (up, right), (down, left), (down, right), (up, w), (down, w)]
    greeted += near + [same_core(k) for k in range(1, nb // 2)]
    for dev in greeted:
        pl.semaphore_signal(barrier, inc=1, device_id=dev, device_id_type=MESH)

    pairs = (
        (lw_hbm, lw_ref), (bits_hbm, bits_ref), (img_hbm, img_ref),
        (log_hbm, both.at[0]), (kern_hbm, kern_ref), (gain_hbm, gain_ref),
    )
    loads = [pltpu.make_async_copy(src, dst, l_sem.at[k]) for k, (src, dst) in enumerate(pairs)]
    for load in loads:
        load.start()
    sblk[:, 8 * JP :, :] = jnp.zeros((LR // 8, QF - 8 * JP, EC), jnp.bfloat16)
    for q in range(4):
        sxblk[QF * q + 8 * JP : QF * q + QF, :] = jnp.zeros((QF - 8 * JP, XL), jnp.bfloat16)
    for load in loads[:3]:
        load.wait()

    rows = lax.broadcasted_iota(jnp.int32, (H, W), 0)
    live0 = jnp.where(img_ref[0, 0, 0, w] < nw, 1.0, 0.0)
    live1 = jnp.where(img_ref[0, 1, 0, w] < nw, 1.0, 0.0)
    weight = lw_ref[...].astype(jnp.bfloat16).astype(jnp.float32)
    weight = weight * jnp.where(rows < TR, live0, live1)
    both[1] = jnp.where(bits_ref[...] == 1, -weight, weight)

    pl.semaphore_wait(barrier, len(greeted))
    for dev in near:
        pl.semaphore_signal(knows_four, inc=1, device_id=dev, device_id_type=MESH)

    def rims(src, dst, send, recv):
        every = slice(None)
        lo, hi = slice(0, HALO), slice(H - HALO, H)
        first, last = slice(0, 128), slice(W - 128, W)
        above, below, mid = slice(0, OWN_R), slice(OWN_R + H, LR), slice(OWN_R, OWN_R + H)
        before, after, centre = slice(0, OWN_C), slice(OWN_C + W, LC), slice(OWN_C, OWN_C + W)
        plan = (
            (lo, first, below, after, (up, left)),
            (lo, last, below, before, (up, right)),
            (hi, first, above, after, (down, left)),
            (hi, last, above, before, (down, right)),
            (lo, slice(0, W), below, centre, (up, w)),
            (hi, slice(0, W), above, centre, (down, w)),
            (slice(0, H), first, mid, after, (b, left)),
            (slice(0, H), last, mid, before, (b, right)),
        )
        copies = []
        for k, (sr, sc, dr, dc, dev) in enumerate(plan):
            copies.append(
                pltpu.make_async_remote_copy(
                    src.at[every, sr, sc], dst.at[every, dr, dc], send.at[k], recv.at[k], dev, MESH
                )
            )
        for copy in copies:
            copy.start()
        return copies

    loads[3].wait()
    copies_a = rims(both, frame, a_send, a_recv)
    frame[:, OWN_R : OWN_R + H, OWN_C : OWN_C + W] = both[...]

    for load in loads[4:]:
        load.wait()
    taps = jnp.transpose(kern_ref[...].astype(jnp.float32).reshape(KS * K2, KS)).astype(jnp.bfloat16)
    lane = lax.broadcasted_iota(jnp.int32, (1, KF), 1)
    channel = (lane >> 3) & 31
    tap = KS - 1 - 8 * (lane >> 8) - (lane & 7)
    source = jnp.where((channel < K2) & (tap >= 0), tap * K2 + channel, -1)
    chosen = lax.broadcasted_iota(jnp.int32, (KS * K2, KF), 0) == source
    chosen = jnp.where(chosen, 1.0, 0.0).astype(jnp.bfloat16)
    base = jnp.dot(taps, chosen, preferred_element_type=jnp.float32)
    lane8 = lax.broadcasted_iota(jnp.int32, (8, KF), 1) & 7
    sub = lax.broadcasted_iota(jnp.int32, (8, KF), 0)
    for j in range(KS):
        row = jnp.broadcast_to(base[j : j + 1, :], (8, KF))
        same = pltpu.roll(row, 0, 1, stride=1, stride_axis=0)
        prior = pltpu.roll(row, QF - 8, 1, stride=1, stride_axis=0)
        wide[8 * j : 8 * j + 8, :] = jnp.where(lane8 >= sub, same, prior)
    wide[8 * KS :, :] = jnp.zeros((QF - 8 * KS, KF), jnp.float32)
    for q in range(4):
        umat[:, QB * q : QB * q + QB] = wide[: 8 * JP, QF * q : QF * q + QB].astype(jnp.bfloat16)
        turned = jnp.transpose(wide[:, QF * (3 - q) : QF * (4 - q)])
        tmat[:, QF * q : QF * q + QF] = turned[:QB].astype(jnp.bfloat16)

    def weights(low, high):
        shape = (high - low, LC)
        band_row = b * H + lax.broadcasted_iota(jnp.int32, shape, 0) + (low - 12)
        band_col = w * W + lax.broadcasted_iota(jnp.int32, shape, 1) - OWN_C
        inside = (band_row >= 0) & (band_row < nb * H) & (band_col >= 0) & (band_col < nw * W)
        signed = jnp.where(inside, frame[1, 12 + low : 12 + high, :], 0.0)
        signed = pltpu.roll(signed, LC - 116, 1)
        vext[low:high, :] = signed[:, :EC]
        vlast[low:high, :] = jnp.where(slot_lane[:, :128] < XC, signed[:, EC : EC + 128], 0.0)

    slot_lane = lax.broadcasted_iota(jnp.int32, (1, LC), 1)
    band_col = w * W + lax.broadcasted_iota(jnp.int32, (8, LC), 1) - OWN_C
    middle = jnp.where((band_col >= 0) & (band_col < nw * W), 1.0, 0.0)
    upper, lower = jnp.where(b > 0, middle, 0.0), jnp.where(b < nb - 1, middle, 0.0)

    sends = list(copies_a)
    for step in range(ITERS):
        def shifted(blk):
            inside = upper if blk < 3 else middle if blk < 9 else lower
            soft = sigmoid(frame[0, 8 * blk : 8 * blk + 8, :])
            rows8 = soft.astype(jnp.bfloat16).astype(jnp.float32) * inside
            last = pltpu.roll(rows8, LC - XAT, 1)[:, :128]
            mlast[8 * blk : 8 * blk + 8, :] = jnp.where(slot_lane[:, :128] < SLOT, last, 0.0)
            rows8 = rows8[:, :XG]
            for j in range(0, JP, 2):
                pair = [pltpu.roll(rows8, XG - 104 - min(j + d, KS - 1), 1)[:, :EC] for d in range(2)]
                sblk[blk, 8 * j : 8 * j + 16, :] = jnp.concatenate(pair, axis=0).astype(jnp.bfloat16)

        def side_by_side(ref, height):
            total = None
            for blk in range(ER // 8):
                part = ref[8 * blk : 8 * blk + height, :]
                part = jnp.concatenate([part, jnp.zeros((height, XL - 128), jnp.float32)], axis=1)
                part = pltpu.roll(part, SLOT * blk, 1) if blk else part
                total = part if total is None else total + part
            return total

        def shifted_last():
            rows32 = side_by_side(mlast, 32)
            for j in range(0, JP, 2):
                pair = []
                for d in range(2):
                    shift = min(j + d, KS - 1)
                    pair.append(pltpu.roll(rows32, XL - shift, 1) if shift else rows32)
                for q in range(4):
                    both8 = [p[8 * q : 8 * q + 8] for p in pair]
                    at = QF * q + 8 * j
                    sxblk[at : at + 16, :] = jnp.concatenate(both8, axis=0).astype(jnp.bfloat16)

        def field_gradient(fields, v, store):
            lanes = v.shape[1]
            fields = fields.reshape(K2, 8, lanes)
            intensity = jnp.zeros((8, lanes), jnp.float32)
            for c in range(K2 // 2):
                f0, f1 = fields[c], fields[c + K2 // 2]
                intensity = intensity + gain_ref[c] * (f0 * f0 + f1 * f1)
            resist = sigmoid(STEEP * (intensity - THRESH))
            target = jnp.where(v < 0.0, 1.0, 0.0)
            slopes = (8.0 * jnp.abs(v)) * (resist - target) * resist * (1.0 - resist)
            for c in range(0, K2, 2):
                pair = [2.0 * gain_ref[(c + d) % (K2 // 2)] * fields[c + d] * slopes for d in range(2)]
                store(8 * c, jnp.concatenate(pair, axis=0))

        def forward(blk):
            window = sblk[blk : blk + 4].reshape(KF, EC)
            fields = jnp.dot(tmat[...], window, preferred_element_type=jnp.float32)

            def store(at, value):
                gblk[blk, at : at + 16, :] = value.astype(jnp.bfloat16)

            field_gradient(fields, vext[8 * blk : 8 * blk + 8, :], store)

        def forward_last():
            fields = jnp.dot(tmat[...], sxblk[...], preferred_element_type=jnp.float32)

            def store(at, value):
                for q in range(4):
                    moved = pltpu.roll(value, XL - SLOT * q, 1) if q else value
                    if XL - SLOT * q < XG:
                        moved = jnp.where(slot_lane < XL - SLOT * q, moved, 0.0)
                    gxblk[QB * q + at : QB * q + at + 16, :] = moved[:, :XG].astype(jnp.bfloat16)

            field_gradient(fields, side_by_side(vlast, 8), store)

        def backward_last():
            spread = jnp.dot(umat[...], gxblk[...], preferred_element_type=jnp.float32)
            spread = spread.reshape(JP, 8, XG)
            total = spread[0]
            for j in range(1, KS):
                total = total + pltpu.roll(spread[j], j, 1)
            lane = lax.broadcasted_iota(jnp.int32, (8, W), 1)
            parts = [pltpu.roll(total, (W - XC - SLOT * k) % XG, 1)[:, :W] for k in range(H // 8)]
            return jnp.concatenate([jnp.where(lane >= W - XC, p, 0.0) for p in parts], axis=0)

        def backward(blk):
            window = gblk[blk : blk + 4].reshape(KB, EC)
            spread = jnp.dot(umat[...], window, preferred_element_type=jnp.float32)
            spread = spread.reshape(JP, 8, EC)
            lane = lax.broadcasted_iota(jnp.int32, (8, EC), 1)
            total = jnp.zeros((8, W), jnp.float32)
            for j in range(KS):
                shift = KS - 1 - j
                moved = pltpu.roll(spread[j], EC - shift, 1) if shift else spread[j]
                total = total + jnp.where(lane < W - shift, moved, 0.0)
            at = OWN_R + blk * 8
            gframe[step, at : at + 8, OWN_C : OWN_C + W] = total

        if step == 0:
            for copy in copies_a[6:]:
                copy.wait_recv()
            weights(24, 48)
        for blk in range(3, 9):
            shifted(blk)
        for blk in range(3, 6):
            forward(blk)
        if step == 0:
            for copy in copies_a[:6]:
                copy.wait_recv()
            pl.semaphore_wait(knows_four, len(near))
            for dev in far:
                pl.semaphore_signal(knows_all, inc=1, device_id=dev, device_id_type=MESH)
            weights(0, 24)
            weights(48, 72)
        for blk in (0, 1, 2):
            shifted(blk)
        for blk in (0, 1, 2):
            forward(blk)
        for blk in (9, 10, 11):
            shifted(blk)
        shifted_last()
        forward_last()
        for blk in (6, 7, 8):
            forward(blk)
        for blk in (0, 1, 2):
            backward(blk)
        last = backward_last()
        for blk in (3, 4, 5):
            backward(blk)

        own = gframe.at[step, OWN_R : OWN_R + H, OWN_C : OWN_C + W]
        own_soft = sigmoid(frame[0, OWN_R : OWN_R + H, OWN_C : OWN_C + W])
        gradient = (own[...] + last) * own_soft * (1.0 - own_soft)
        own[...] = gradient
        if step < ITERS - 1:
            copies_g = rims(gframe.at[pl.ds(step, 1), OWN_R : OWN_R + H, OWN_C : OWN_C + W], gframe.at[pl.ds(step, 1)], g_send, g_recv)
            sends += copies_g

        squares = jnp.sum(gradient * gradient, axis=0, keepdims=True)
        squares = squares[:, :128] + squares[:, 128:]

        def reduce(value, at, slots, order, me, device):
            count = len(order) + 1
            part[at] = value
            slots[step, pl.ds(me, 1)] = value[None]
            for k in order:
                pltpu.make_async_remote_copy(
                    part.at[at], slots.at[step, me], r_send.at[at], r_recv.at[at], device(k), MESH
                ).start()
            peers = slots.at[step, pl.ds(0, count - 1)]
            every = pltpu.make_async_remote_copy(
                peers, peers, r_send.at[at], r_recv.at[at], device(1), MESH
            )
            every.wait_recv()
            return jnp.sum(slots[step], axis=0), every

        stages = (
            (slots_c, [1], core, other_core),
            (slots_b, farthest_first(nb // 8, 4), b // 2, same_core),
            (slots_w, farthest_first(nw), w, along_work),
        )
        for at, (slots, order, me, device) in enumerate(stages):
            if step == 0 and at == len(stages) - 1:
                pl.semaphore_wait(knows_all, len(far))
            squares, every = reduce(squares, 3 * step + at, slots, order, me, device)
            sends.append(every)
        mean = jnp.sum(squares, axis=1, keepdims=True) * (1.0 / (nb * nw * H * W))
        scale = STEP_SIZE / jnp.sqrt(mean + EPSILON)
        if step < ITERS - 1:
            for copy in copies_g:
                copy.wait_recv()
            frame[0] = frame[0] - scale * gframe[step]
        else:
            out_ref[...] = frame[0, OWN_R : OWN_R + H, OWN_C : OWN_C + W] - scale * gradient
    for copy in sends:
        copy.wait_send()


def solution(mesh):
    nb, nw = mesh.shape["band"], mesh.shape["work"]

    def shards(mask_logits, loss_weights, target_bits, kernels, kernel_gains, imager_list):
        operands = (
            mask_logits,
            loss_weights,
            target_bits,
            jnp.transpose(kernels, (1, 0, 2)),
            kernel_gains,
            jnp.transpose(imager_list, (0, 2, 3, 1)),
        )
        vmem = pl.BlockSpec(memory_space=pltpu.VMEM)
        hbm = pl.BlockSpec(memory_space=pltpu.HBM)
        dma = pltpu.SemaphoreType.DMA
        return pl.pallas_call(
            functools.partial(kernel, nb, nw),
            out_shape=jax.ShapeDtypeStruct((H, W), jnp.float32),
            in_specs=[hbm] * 6,
            out_specs=vmem,
            scratch_shapes=[
                pltpu.VMEM((H, W), jnp.float32),
                pltpu.VMEM((H, W), jnp.int32),
                pltpu.VMEM((KS, K2, KS), jnp.bfloat16),
                pltpu.SMEM((K2 // 2,), jnp.float32),
                pltpu.SMEM((1, H // TR, 1, nw), jnp.int32),
                pltpu.VMEM((2, H, W), jnp.float32),
                pltpu.VMEM((2, LR, LC), jnp.float32),
                pltpu.VMEM((ITERS, LR, LC), jnp.float32),
                pltpu.VMEM((ER, EC), jnp.float32),
                pltpu.VMEM((ER, 128), jnp.float32),
                pltpu.VMEM((LR, 128), jnp.float32),
                pltpu.VMEM((QF, KF), jnp.float32),
                pltpu.VMEM((QB, KF), jnp.bfloat16),
                pltpu.VMEM((JP * 8, KB), jnp.bfloat16),
                pltpu.VMEM((LR // 8, QF, EC), jnp.bfloat16),
                pltpu.VMEM((KF, XL), jnp.bfloat16),
                pltpu.VMEM((ER // 8, QB, EC), jnp.bfloat16),
                pltpu.VMEM((KB, XG), jnp.bfloat16),
                pltpu.VMEM((ITERS, 2, 1, 128), jnp.float32),
                pltpu.VMEM((ITERS, nb // 2, 1, 128), jnp.float32),
                pltpu.VMEM((ITERS, nw, 1, 128), jnp.float32),
                pltpu.VMEM((3 * ITERS, 1, 128), jnp.float32),
                dma((6,)), dma((8,)), dma((8,)), dma((8,)), dma((8,)),
                dma((3 * ITERS,)), dma((3 * ITERS,)),
                pltpu.SemaphoreType.REGULAR, pltpu.SemaphoreType.REGULAR,
            ],
            compiler_params=pltpu.CompilerParams(
                collective_id=0, has_side_effects=True, vmem_limit_bytes=40 * 1024 * 1024
            ),
        )(
            *[pltpu.with_memory_space_constraint(operand, pltpu.HBM) for operand in operands]
        )

    in_specs = (
        P("band", "work"),
        P("band", "work"),
        P("band", "work"),
        P(),
        P(),
        P("band", None, None, None),
    )
    return jax.shard_map(
        shards, mesh=mesh, in_specs=in_specs, out_specs=P("band", "work"), check_vma=False
    )
```

```python
import functools

import jax
import jax.numpy as jnp
from jax import lax
from jax.experimental import pallas as pl
from jax.experimental.pallas import tpu as pltpu
from jax.sharding import PartitionSpec as P

MESH = pl.DeviceIdType.MESH
TR = 24
H, W = 48, 256
K2 = 24
KS = 25
JP = 26
HALO = 24
ER, EC = 72, 256
XC = 24
SLOT, XL, XG = 48, 512, 384
XAT = 104 + EC
LR, LC = 96, 512
OWN_R, OWN_C = 24, 128
QF, QB = 256, 192
KF, KB = 4 * QF, 4 * QB
ITERS = 2
STEEP, THRESH, STEP_SIZE, EPSILON = 4.0, 0.5, 0.5, 1e-6


def farthest_first(*rings):
    count = 1
    for ring in rings:
        count *= ring

    def links(k):
        total = 0
        for ring in reversed(rings):
            total += min(k % ring, ring - k % ring)
            k //= ring
        return total

    return sorted(range(1, count), key=lambda k: -links(k))


def sigmoid(x):
    return 1.0 / (1.0 + jnp.exp(-x))


def kernel(
    nb, nw, log_hbm, lw_hbm, bits_hbm, kern_hbm, gain_hbm, img_hbm, out_ref,
    lw_ref, bits_ref, kern_ref, gain_ref, img_ref,
    both, frame, gframe, vext, vlast, mlast, wide, tmat, umat, sblk, sxblk, gblk, gxblk,
    slots_c, slots_b, slots_w, part,
    l_sem, a_send, a_recv, g_send, g_recv, r_send, r_recv, knows_four, knows_all,
):
    b, w = lax.axis_index("band"), lax.axis_index("work")
    up, down = lax.rem(b + nb - 1, nb), lax.rem(b + 1, nb)
    left, right = lax.rem(w + nw - 1, nw), lax.rem(w + 1, nw)

    core = lax.rem(b, 2)

    def other_core(k):
        return (b + 1 - 2 * core, w)

    def same_core(k):
        return (lax.rem(b + 2 * k, nb), w)

    def along_work(k):
        return (b, lax.rem(w + k, nw))

    barrier = pltpu.get_barrier_semaphore()
    near = [along_work(k) for k in (1, 2, nw - 2, nw - 1)]
    far = [along_work(k) for k in (3, 4, nw - 4, nw - 3)]
    greeted = [(up, left), (up, right), (down, left), (down, right), (up, w), (down, w)]
    greeted += near + [same_core(k) for k in range(1, nb // 2)]
    for dev in greeted:
        pl.semaphore_signal(barrier, inc=1, device_id=dev, device_id_type=MESH)

    pairs = (
        (lw_hbm, lw_ref), (bits_hbm, bits_ref), (img_hbm, img_ref),
        (log_hbm, both.at[0]), (kern_hbm, kern_ref), (gain_hbm, gain_ref),
    )
    loads = [pltpu.make_async_copy(src, dst, l_sem.at[k]) for k, (src, dst) in enumerate(pairs)]
    for load in loads:
        load.start()
    sblk[:, 8 * JP :, :] = jnp.zeros((LR // 8, QF - 8 * JP, EC), jnp.bfloat16)
    for q in range(4):
        sxblk[QF * q + 8 * JP : QF * q + QF, :] = jnp.zeros((QF - 8 * JP, XL), jnp.bfloat16)
    for load in loads[:3]:
        load.wait()

    rows = lax.broadcasted_iota(jnp.int32, (H, W), 0)
    live0 = jnp.where(img_ref[0, 0, 0, w] < nw, 1.0, 0.0)
    live1 = jnp.where(img_ref[0, 1, 0, w] < nw, 1.0, 0.0)
    weight = lw_ref[...].astype(jnp.bfloat16).astype(jnp.float32)
    weight = weight * jnp.where(rows < TR, live0, live1)
    both[1] = jnp.where(bits_ref[...] == 1, -weight, weight)

    pl.semaphore_wait(barrier, len(greeted))
    for dev in near:
        pl.semaphore_signal(knows_four, inc=1, device_id=dev, device_id_type=MESH)

    def rims(src, dst, send, recv):
        every = slice(None)
        lo, hi = slice(0, HALO), slice(H - HALO, H)
        first, last = slice(0, 128), slice(W - 128, W)
        above, below, mid = slice(0, OWN_R), slice(OWN_R + H, LR), slice(OWN_R, OWN_R + H)
        before, after, centre = slice(0, OWN_C), slice(OWN_C + W, LC), slice(OWN_C, OWN_C + W)
        plan = (
            (lo, first, below, after, (up, left)),
            (lo, last, below, before, (up, right)),
            (hi, first, above, after, (down, left)),
            (hi, last, above, before, (down, right)),
            (lo, slice(0, W), below, centre, (up, w)),
            (hi, slice(0, W), above, centre, (down, w)),
            (slice(0, H), first, mid, after, (b, left)),
            (slice(0, H), last, mid, before, (b, right)),
        )
        copies = []
        for k, (sr, sc, dr, dc, dev) in enumerate(plan):
            copies.append(
                pltpu.make_async_remote_copy(
                    src.at[every, sr, sc], dst.at[every, dr, dc], send.at[k], recv.at[k], dev, MESH
                )
            )
        for copy in copies:
            copy.start()
        return copies

    loads[3].wait()
    copies_a = rims(both, frame, a_send, a_recv)
    frame[:, OWN_R : OWN_R + H, OWN_C : OWN_C + W] = both[...]

    for load in loads[4:]:
        load.wait()
    taps = jnp.transpose(kern_ref[...].astype(jnp.float32).reshape(KS * K2, KS)).astype(jnp.bfloat16)
    lane = lax.broadcasted_iota(jnp.int32, (1, KF), 1)
    channel = (lane >> 3) & 31
    tap = KS - 1 - 8 * (lane >> 8) - (lane & 7)
    source = jnp.where((channel < K2) & (tap >= 0), tap * K2 + channel, -1)
    chosen = lax.broadcasted_iota(jnp.int32, (KS * K2, KF), 0) == source
    chosen = jnp.where(chosen, 1.0, 0.0).astype(jnp.bfloat16)
    base = jnp.dot(taps, chosen, preferred_element_type=jnp.float32)
    lane8 = lax.broadcasted_iota(jnp.int32, (8, KF), 1) & 7
    sub = lax.broadcasted_iota(jnp.int32, (8, KF), 0)
    for j in range(KS):
        row = jnp.broadcast_to(base[j : j + 1, :], (8, KF))
        same = pltpu.roll(row, 0, 1, stride=1, stride_axis=0)
        prior = pltpu.roll(row, QF - 8, 1, stride=1, stride_axis=0)
        wide[8 * j : 8 * j + 8, :] = jnp.where(lane8 >= sub, same, prior)
    wide[8 * KS :, :] = jnp.zeros((QF - 8 * KS, KF), jnp.float32)
    for q in range(4):
        umat[:, QB * q : QB * q + QB] = wide[: 8 * JP, QF * q : QF * q + QB].astype(jnp.bfloat16)
        turned = jnp.transpose(wide[:, QF * (3 - q) : QF * (4 - q)])
        tmat[:, QF * q : QF * q + QF] = turned[:QB].astype(jnp.bfloat16)

    def weights(low, high):
        shape = (high - low, LC)
        band_row = b * H + lax.broadcasted_iota(jnp.int32, shape, 0) + (low - 12)
        band_col = w * W + lax.broadcasted_iota(jnp.int32, shape, 1) - OWN_C
        inside = (band_row >= 0) & (band_row < nb * H) & (band_col >= 0) & (band_col < nw * W)
        signed = jnp.where(inside, frame[1, 12 + low : 12 + high, :], 0.0)
        signed = pltpu.roll(signed, LC - 116, 1)
        vext[low:high, :] = signed[:, :EC]
        vlast[low:high, :] = jnp.where(slot_lane[:, :128] < XC, signed[:, EC : EC + 128], 0.0)

    slot_lane = lax.broadcasted_iota(jnp.int32, (1, LC), 1)
    band_col = w * W + lax.broadcasted_iota(jnp.int32, (8, LC), 1) - OWN_C
    middle = jnp.where((band_col >= 0) & (band_col < nw * W), 1.0, 0.0)
    upper, lower = jnp.where(b > 0, middle, 0.0), jnp.where(b < nb - 1, middle, 0.0)

    sends = list(copies_a)
    for step in range(ITERS):
        def shifted(blk):
            inside = upper if blk < 3 else middle if blk < 9 else lower
            soft = sigmoid(frame[0, 8 * blk : 8 * blk + 8, :])
            rows8 = soft.astype(jnp.bfloat16).astype(jnp.float32) * inside
            last = pltpu.roll(rows8, LC - XAT, 1)[:, :128]
            mlast[8 * blk : 8 * blk + 8, :] = jnp.where(slot_lane[:, :128] < SLOT, last, 0.0)
            rows8 = rows8[:, :XG]
            for j in range(0, JP, 2):
                pair = [pltpu.roll(rows8, XG - 104 - min(j + d, KS - 1), 1)[:, :EC] for d in range(2)]
                sblk[blk, 8 * j : 8 * j + 16, :] = jnp.concatenate(pair, axis=0).astype(jnp.bfloat16)

        def side_by_side(ref, height):
            total = None
            for blk in range(ER // 8):
                part = ref[8 * blk : 8 * blk + height, :]
                part = jnp.concatenate([part, jnp.zeros((height, XL - 128), jnp.float32)], axis=1)
                part = pltpu.roll(part, SLOT * blk, 1) if blk else part
                total = part if total is None else total + part
            return total

        def shifted_last():
            rows32 = side_by_side(mlast, 32)
            for j in range(0, JP, 2):
                pair = []
                for d in range(2):
                    shift = min(j + d, KS - 1)
                    pair.append(pltpu.roll(rows32, XL - shift, 1) if shift else rows32)
                for q in range(4):
                    both8 = [p[8 * q : 8 * q + 8] for p in pair]
                    at = QF * q + 8 * j
                    sxblk[at : at + 16, :] = jnp.concatenate(both8, axis=0).astype(jnp.bfloat16)

        def field_gradient(fields, v, store):
            lanes = v.shape[1]
            fields = fields.reshape(K2, 8, lanes)
            intensity = jnp.zeros((8, lanes), jnp.float32)
            for c in range(K2 // 2):
                f0, f1 = fields[c], fields[c + K2 // 2]
                intensity = intensity + gain_ref[c] * (f0 * f0 + f1 * f1)
            resist = sigmoid(STEEP * (intensity - THRESH))
            target = jnp.where(v < 0.0, 1.0, 0.0)
            slopes = (8.0 * jnp.abs(v)) * (resist - target) * resist * (1.0 - resist)
            for c in range(0, K2, 2):
                pair = [2.0 * gain_ref[(c + d) % (K2 // 2)] * fields[c + d] * slopes for d in range(2)]
                store(8 * c, jnp.concatenate(pair, axis=0))

        def forward(blk):
            window = sblk[blk : blk + 4].reshape(KF, EC)
            fields = jnp.dot(tmat[...], window, preferred_element_type=jnp.float32)

            def store(at, value):
                gblk[blk, at : at + 16, :] = value.astype(jnp.bfloat16)

            field_gradient(fields, vext[8 * blk : 8 * blk + 8, :], store)

        def forward_last():
            fields = jnp.dot(tmat[...], sxblk[...], preferred_element_type=jnp.float32)

            def store(at, value):
                for q in range(4):
                    moved = pltpu.roll(value, XL - SLOT * q, 1) if q else value
                    if XL - SLOT * q < XG:
                        moved = jnp.where(slot_lane < XL - SLOT * q, moved, 0.0)
                    gxblk[QB * q + at : QB * q + at + 16, :] = moved[:, :XG].astype(jnp.bfloat16)

            field_gradient(fields, side_by_side(vlast, 8), store)

        def backward_last():
            spread = jnp.dot(umat[...], gxblk[...], preferred_element_type=jnp.float32)
            spread = spread.reshape(JP, 8, XG)
            total = spread[0]
            for j in range(1, KS):
                total = total + pltpu.roll(spread[j], j, 1)
            lane = lax.broadcasted_iota(jnp.int32, (8, W), 1)
            parts = [pltpu.roll(total, (W - XC - SLOT * k) % XG, 1)[:, :W] for k in range(H // 8)]
            return jnp.concatenate([jnp.where(lane >= W - XC, p, 0.0) for p in parts], axis=0)

        def backward(blk):
            window = gblk[blk : blk + 4].reshape(KB, EC)
            spread = jnp.dot(umat[...], window, preferred_element_type=jnp.float32)
            spread = spread.reshape(JP, 8, EC)
            lane = lax.broadcasted_iota(jnp.int32, (8, EC), 1)
            total = jnp.zeros((8, W), jnp.float32)
            for j in range(KS):
                shift = KS - 1 - j
                moved = pltpu.roll(spread[j], EC - shift, 1) if shift else spread[j]
                total = total + jnp.where(lane < W - shift, moved, 0.0)
            at = OWN_R + blk * 8
            gframe[step, at : at + 8, OWN_C : OWN_C + W] = total

        if step == 0:
            for copy in copies_a[6:]:
                copy.wait_recv()
            weights(24, 48)
        for blk in range(3, 9):
            shifted(blk)
        for blk in range(3, 6):
            forward(blk)
        if step == 0:
            for copy in copies_a[:6]:
                copy.wait_recv()
            pl.semaphore_wait(knows_four, len(near))
            for dev in far:
                pl.semaphore_signal(knows_all, inc=1, device_id=dev, device_id_type=MESH)
            weights(0, 24)
            weights(48, 72)
        for blk in (0, 1, 2):
            shifted(blk)
        for blk in (0, 1, 2):
            forward(blk)
        for blk in (9, 10, 11):
            shifted(blk)
        shifted_last()
        forward_last()
        for blk in (6, 7, 8):
            forward(blk)
        for blk in (0, 1, 2):
            backward(blk)
        last = backward_last()
        for blk in (3, 4, 5):
            backward(blk)

        own = gframe.at[step, OWN_R : OWN_R + H, OWN_C : OWN_C + W]
        own_soft = sigmoid(frame[0, OWN_R : OWN_R + H, OWN_C : OWN_C + W])
        gradient = (own[...] + last) * own_soft * (1.0 - own_soft)
        own[...] = gradient
        squares = jnp.sum(gradient * gradient, axis=0, keepdims=True)
        squares = squares[:, :128] + squares[:, 128:]

        def reduce(value, at, slots, order, me, device):
            count = len(order) + 1
            part[at] = value
            slots[step, pl.ds(me, 1)] = value[None]
            for k in order:
                pltpu.make_async_remote_copy(
                    part.at[at], slots.at[step, me], r_send.at[at], r_recv.at[at], device(k), MESH
                ).start()
            peers = slots.at[step, pl.ds(0, count - 1)]
            every = pltpu.make_async_remote_copy(
                peers, peers, r_send.at[at], r_recv.at[at], device(1), MESH
            )
            every.wait_recv()
            return jnp.sum(slots[step], axis=0), every

        stages = (
            (slots_c, [1], core, other_core),
            (slots_b, farthest_first(nb // 8, 4), b // 2, same_core),
            (slots_w, farthest_first(nw), w, along_work),
        )
        for at, (slots, order, me, device) in enumerate(stages):
            if step == 0 and at == len(stages) - 1:
                pl.semaphore_wait(knows_all, len(far))
            squares, every = reduce(squares, 3 * step + at, slots, order, me, device)
            sends.append(every)
            if at == 0 and step < ITERS - 1:
                copies_g = rims(gframe.at[pl.ds(step, 1), OWN_R : OWN_R + H, OWN_C : OWN_C + W], gframe.at[pl.ds(step, 1)], g_send, g_recv)
                sends += copies_g
        mean = jnp.sum(squares, axis=1, keepdims=True) * (1.0 / (nb * nw * H * W))
        scale = STEP_SIZE / jnp.sqrt(mean + EPSILON)
        if step < ITERS - 1:
            for copy in copies_g:
                copy.wait_recv()
            frame[0] = frame[0] - scale * gframe[step]
        else:
            out_ref[...] = frame[0, OWN_R : OWN_R + H, OWN_C : OWN_C + W] - scale * gradient
    for copy in sends:
        copy.wait_send()


def solution(mesh):
    nb, nw = mesh.shape["band"], mesh.shape["work"]

    def shards(mask_logits, loss_weights, target_bits, kernels, kernel_gains, imager_list):
        operands = (
            mask_logits,
            loss_weights,
            target_bits,
            jnp.transpose(kernels, (1, 0, 2)),
            kernel_gains,
            jnp.transpose(imager_list, (0, 2, 3, 1)),
        )
        vmem = pl.BlockSpec(memory_space=pltpu.VMEM)
        hbm = pl.BlockSpec(memory_space=pltpu.HBM)
        dma = pltpu.SemaphoreType.DMA
        return pl.pallas_call(
            functools.partial(kernel, nb, nw),
            out_shape=jax.ShapeDtypeStruct((H, W), jnp.float32),
            in_specs=[hbm] * 6,
            out_specs=vmem,
            scratch_shapes=[
                pltpu.VMEM((H, W), jnp.float32),
                pltpu.VMEM((H, W), jnp.int32),
                pltpu.VMEM((KS, K2, KS), jnp.bfloat16),
                pltpu.SMEM((K2 // 2,), jnp.float32),
                pltpu.SMEM((1, H // TR, 1, nw), jnp.int32),
                pltpu.VMEM((2, H, W), jnp.float32),
                pltpu.VMEM((2, LR, LC), jnp.float32),
                pltpu.VMEM((ITERS, LR, LC), jnp.float32),
                pltpu.VMEM((ER, EC), jnp.float32),
                pltpu.VMEM((ER, 128), jnp.float32),
                pltpu.VMEM((LR, 128), jnp.float32),
                pltpu.VMEM((QF, KF), jnp.float32),
                pltpu.VMEM((QB, KF), jnp.bfloat16),
                pltpu.VMEM((JP * 8, KB), jnp.bfloat16),
                pltpu.VMEM((LR // 8, QF, EC), jnp.bfloat16),
                pltpu.VMEM((KF, XL), jnp.bfloat16),
                pltpu.VMEM((ER // 8, QB, EC), jnp.bfloat16),
                pltpu.VMEM((KB, XG), jnp.bfloat16),
                pltpu.VMEM((ITERS, 2, 1, 128), jnp.float32),
                pltpu.VMEM((ITERS, nb // 2, 1, 128), jnp.float32),
                pltpu.VMEM((ITERS, nw, 1, 128), jnp.float32),
                pltpu.VMEM((3 * ITERS, 1, 128), jnp.float32),
                dma((6,)), dma((8,)), dma((8,)), dma((8,)), dma((8,)),
                dma((3 * ITERS,)), dma((3 * ITERS,)),
                pltpu.SemaphoreType.REGULAR, pltpu.SemaphoreType.REGULAR,
            ],
            compiler_params=pltpu.CompilerParams(
                collective_id=0, has_side_effects=True, vmem_limit_bytes=40 * 1024 * 1024
            ),
        )(
            *[pltpu.with_memory_space_constraint(operand, pltpu.HBM) for operand in operands]
        )

    in_specs = (
        P("band", "work"),
        P("band", "work"),
        P("band", "work"),
        P(),
        P(),
        P("band", None, None, None),
    )
    return jax.shard_map(
        shards, mesh=mesh, in_specs=in_specs, out_specs=P("band", "work"), check_vma=False
    )
```
